512 devices in a mesh: dp: 32 (over z, core), space: 16 (over x, y).
Axes of the slice: x: 4, y: 4, z: 16, core: 2. Of those that a mesh axis runs over, the one named last changes fastest.
Arguments:
- inputs: bfloat16 [32, 256, 9216], P('dp', 'space'), may hold values from -6 to 6
- cotangent: bfloat16 [32, 256, 9216], P('dp', 'space'), may hold values from -6 to 6
- weights: bfloat16 [3, 9, 36864], replicated, may hold values from -0.15625 to 0.15625
Outputs:
- outputs: bfloat16 [32, 256, 9216], P('dp', 'space')
- input_grad: bfloat16 [32, 256, 9216], P('dp', 'space')
- weight_grad: float32 [27, 36864], P(None, ('dp', 'space'))
The draws below stay inside these ranges and needn't reach their ends.
All inputs are finite; a program needn't handle non-finite values.
Results may differ from the reference program's by a relative error of at most 0.014.
Values may be sent and summed in bfloat16 or wider, within the bound.
No kernel may reach another device: no remote copies, remote signals or barrier semaphores. Data moves between devices by JAX's collectives and lax.ppermute only.
A program may use at most 128 MiB of HBM per device.

```python
import math
import jax
import jax.numpy as jnp
from jax import lax

CHANNELS = 192
ROWS_DEV = 16
WIDTH = 48
LAYERS = 3
SAMPLES = 32
HEIGHT = 256


def shard_levels(key, dims, split, least, high):
    def one(axis_at, blocks):
        heights = jax.random.uniform(jax.random.fold_in(jax.random.fold_in(key, 6), axis_at), (blocks,), jnp.float32, least / len(split), high / len(split))
        return jnp.repeat(jnp.exp(heights), dims[axis_at] // blocks).reshape((-1,) + (1,) * (len(dims) - axis_at - 1))

    level = one(*split[0])
    for cut in split[1:]:
        level = level * one(*cut)
    return level


def noise(rng, shape, width, limit, cuts=(), kind=jnp.bfloat16):
    loudness = shard_levels(rng, shape, cuts, -0.22, 0.18) if cuts else 1.0
    result = jax.random.normal(rng, shape, jnp.float32) * width * loudness
    return jnp.minimum(jnp.maximum(result, -limit), limit).astype(kind)


def setup_inputs(seed: int = 0) -> dict:
    keys = jax.random.split(jax.random.key(seed), 4)
    return {
        "inputs": noise(keys[0], (SAMPLES, HEIGHT, WIDTH * CHANNELS), 1.0, 6.0, ((0, 32), (1, 16))),
        "cotangent": noise(keys[1], (SAMPLES, HEIGHT, WIDTH * CHANNELS), 1.0, 6.0, ((0, 32), (1, 16))),
        "weights": noise(keys[2], (LAYERS, 9, CHANNELS * CHANNELS), (9 * CHANNELS) ** -0.5, 0.15625),
    }


def row_slide(values, offset):
    extent = values.shape[0]
    if offset == 0:
        return values
    if abs(offset) >= extent:
        return jnp.zeros_like(values)
    filler = jnp.zeros((abs(offset),) + values.shape[1:], values.dtype)
    if offset > 0:
        return jnp.concatenate([values[offset:], filler], 0)
    return jnp.concatenate([filler, values[:offset]], 0)

def column_slide(values, offset):
    extent = values.shape[1]
    if offset == 0:
        return values
    if abs(offset) >= extent:
        return jnp.zeros_like(values)
    filler = jnp.zeros((values.shape[0], abs(offset)) + values.shape[2:], values.dtype)
    if offset > 0:
        return jnp.concatenate([values[:, offset:], filler], 1)
    return jnp.concatenate([filler, values[:, :offset]], 1)

def convolve(beside_all, kernel, spread):
    channel_count = kernel.shape[1]
    summed = jnp.zeros(beside_all[1].shape, jnp.float32)
    for i in range(3):
        for j in range(3):
            shifted = column_slide(beside_all[i], (j - 1) * spread).reshape(-1, channel_count)
            summed = summed + jnp.dot(shifted, kernel[3 * i + j], preferred_element_type=jnp.float32).reshape(summed.shape)
    return summed

def convolve_back(beside_all, kernel, spread):
    channel_count = kernel.shape[1]
    summed = jnp.zeros(beside_all[1].shape, jnp.float32)
    for i in range(3):
        for j in range(3):
            shifted = column_slide(beside_all[2 - i], (1 - j) * spread).reshape(-1, channel_count)
            summed = summed + jnp.dot(shifted, kernel[3 * i + j].T, preferred_element_type=jnp.float32).reshape(summed.shape)
    return summed

def kernel_grad(beside_all, upstream, spread):
    channel_count = upstream.shape[-1]
    flat_up = upstream.reshape(-1, channel_count)
    pieces = []
    for i in range(3):
        for j in range(3):
            shifted = column_slide(beside_all[i], (j - 1) * spread).reshape(-1, channel_count)
            pieces.append(jnp.dot(shifted.T, flat_up, preferred_element_type=jnp.float32).reshape(-1))
    return jnp.stack(pieces)

def gelu_slope(values):
    return jax.vjp(jax.nn.gelu, values)[1](jnp.ones_like(values))[0]

def one_sample(sample, upstream, weights):
    kernels = weights.reshape(LAYERS, 9, CHANNELS, CHANNELS)
    spreads = (1, ROWS_DEV, 2 * ROWS_DEV)
    current = sample.reshape(HEIGHT, WIDTH, CHANNELS)
    saved_states = []
    saved_acts = []
    for layer_index in range(LAYERS):
        spread = spreads[layer_index]
        active = jax.nn.gelu(current.astype(jnp.float32)).astype(jnp.bfloat16)
        beside_all = (row_slide(active, -spread), active, row_slide(active, spread))
        branch = convolve(beside_all, kernels[layer_index], spread)
        saved_states.append(current)
        saved_acts.append(beside_all)
        current = (current.astype(jnp.float32) + branch).astype(jnp.bfloat16)
    gradient = upstream.reshape(HEIGHT, WIDTH, CHANNELS)
    layer_grads = [None] * LAYERS
    for layer_index in reversed(range(LAYERS)):
        spread = spreads[layer_index]
        around_grad = (row_slide(gradient, -spread), gradient, row_slide(gradient, spread))
        backward_term = convolve_back(around_grad, kernels[layer_index], spread)
        layer_grads[layer_index] = kernel_grad(saved_acts[layer_index], gradient, spread)
        slope = gelu_slope(saved_states[layer_index].astype(jnp.float32))
        gradient = (gradient.astype(jnp.float32) + backward_term * slope).astype(jnp.bfloat16)
    return (current.reshape(HEIGHT, WIDTH * CHANNELS), gradient.reshape(HEIGHT, WIDTH * CHANNELS), jnp.concatenate(layer_grads, 0))

def reference(inputs, cotangent, weights):

    def sample_step(sample_pair):
        return one_sample(sample_pair[0], sample_pair[1], weights)
    outputs, input_grad, per_sample = lax.map(sample_step, (inputs, cotangent))
    grad_scale = 1.0 / math.sqrt(SAMPLES * HEIGHT * WIDTH)
    weight_grad = lax.optimization_barrier(jnp.sum(per_sample, axis=0)) * grad_scale
    return (outputs, input_grad, weight_grad)
```

```python
import math

import jax
import jax.numpy as jnp
from jax import lax
from jax.experimental import pallas as pl
from jax.experimental.pallas import tpu as pltpu
from jax.sharding import Mesh
from jax.sharding import PartitionSpec as P


DP = ("z", "core")
SPACE = ("x", "y")
CH = 192
ROWS = 16
WIDTH = 48
HEIGHT = 256
GROUPS = 3
CELLS = GROUPS * HEIGHT
F32 = jnp.float32
BF16 = jnp.bfloat16
GELU_A = math.sqrt(2.0 / math.pi)
GELU_B = 0.044715
VMEM_LIMIT = 24 * 1024 * 1024


def gelu(x):
    return x * (0.5 * (1.0 + jnp.tanh(GELU_A * (x + GELU_B * (x * x * x)))))


def gelu_and_slope(x):
    square = x * x
    tanh = jnp.tanh(GELU_A * (x + GELU_B * (x * square)))
    cdf = 0.5 * (1.0 + tanh)
    slope = cdf + (0.5 * x) * ((1.0 - tanh * tanh) * (GELU_A + (3.0 * GELU_A * GELU_B) * square))
    return x * cdf, slope


def dot(a, b):
    return lax.dot_general(a, b, (((1,), (0,)), ((), ())), preferred_element_type=F32)


def dot_t(a, b):
    return lax.dot_general(a, b, (((1,), (1,)), ((), ())), preferred_element_type=F32)


def call(kernel, out_shape, *args, scratch=(), flops=0, moved=0, after=()):
    return pl.pallas_call(
        kernel,
        out_shape=out_shape,
        in_specs=[pl.BlockSpec(memory_space=pltpu.VMEM)] * len(args)
        + [pl.BlockSpec(memory_space=pl.ANY)] * len(after),
        out_specs=jax.tree.map(lambda _: pl.BlockSpec(memory_space=pltpu.VMEM), out_shape),
        scratch_shapes=list(scratch),
        compiler_params=pltpu.CompilerParams(vmem_limit_bytes=VMEM_LIMIT),
        cost_estimate=pl.CostEstimate(flops=flops, bytes_accessed=moved, transcendentals=0),
    )(*args, *after)


def shape(*dims, dtype=BF16):
    return jax.ShapeDtypeStruct(dims, dtype)


def pack_kernel(x_hbm, c_hbm, send_ref, x_ref, c_ref, act_ref, sems):
    copies = [
        pltpu.make_async_copy(x_hbm, x_ref, sems.at[0]),
        pltpu.make_async_copy(c_hbm, c_ref, sems.at[1]),
    ]
    for copy in copies:
        copy.start()
    for copy in copies:
        copy.wait()
    act_ref[...] = gelu(x_ref[0].astype(F32)).astype(BF16)

    def column(load, w):
        pair = load(384 * (w // 2))
        base = 192 * (w % 2)
        return pair[:, base : base + 128], pair[:, base + 128 : base + 192]

    nothing = jnp.zeros((16, 128), BF16), jnp.zeros((16, 64), BF16)
    act, raw, cot = [], [], []
    for w in range(WIDTH):
        act.append(column(lambda at: act_ref[:, at : at + 384], w))
        raw.append(column(lambda at: x_ref[0, :, at : at + 384], w))
        cot.append(column(lambda at: c_ref[0, :, at : at + 384], w))
    for b in range(16):
        blocks = []
        for g in range(4):
            for a in range(GROUPS):
                w = 16 * a + b
                if g == 0:
                    blocks.append(act[w - 1] if w > 0 else nothing)
                elif g == 1:
                    blocks.append(raw[w])
                elif g == 2:
                    blocks.append(act[w + 1] if w < WIDTH - 1 else nothing)
                else:
                    blocks.append(cot[w])
        for k in range(12):
            send_ref[b, 16 * k : 16 * k + 16, :] = blocks[k][0]
        for k in range(6):
            both = jnp.concatenate([blocks[2 * k][1], blocks[2 * k + 1][1]], axis=1)
            send_ref[b, 192 + 16 * k : 208 + 16 * k, :] = both


def shifted_rows(value, by):
    rows = lax.broadcasted_iota(jnp.int32, value.shape, 0)
    rolled = pltpu.roll(value, (-by) % value.shape[0], 0)
    keep = rows != (0 if by < 0 else value.shape[0] - 1)
    return jnp.where(keep, rolled, 0.0)


def spread_conv(padded, w_ref, layer, width, step, transposed):
    totals = [None] * GROUPS
    for j in range(3):
        off = (1 - j) * step if transposed else (j - 1) * step
        outs = [a for a in range(GROUPS) if 0 <= a + off < GROUPS]
        lo, n = outs[0], len(outs)
        total = None
        for i in range(3):
            at = width * (2 - i) if transposed else width * i
            cells = padded[lo + off : lo + off + n, at : at + HEIGHT, :].reshape(n * HEIGHT, CH)
            kernel = w_ref[9 * layer + 3 * i + j]
            term = dot_t(cells, kernel) if transposed else dot(cells, kernel)
            total = term if total is None else total + term
        for m, a in enumerate(outs):
            part = total[m * HEIGHT : (m + 1) * HEIGHT]
            totals[a] = part if totals[a] is None else totals[a] + part
    return totals


def clear_edges(ref, pad):
    for a in range(GROUPS):
        ref[a, 0:pad, :] = jnp.zeros((pad, CH), BF16)
        ref[a, pad + HEIGHT : 2 * pad + HEIGHT, :] = jnp.zeros((pad, CH), BF16)


def main_kernel(
    recv_ref, w_ref, a0_ref, a1_ref, a2_ref, g1_ref, g2_ref, g3_ref, s2_ref,
    a1p, g2p, g3p, slope1, slope2,
):
    def block(k):
        lo = recv_ref[:, 16 * k : 16 * k + 16, :].reshape(HEIGHT, 128)
        at = 192 + 16 * (k // 2)
        hi = recv_ref[:, at : at + 16, :].reshape(HEIGHT, 128)[:, 64 * (k % 2) : 64 * (k % 2) + 64]
        return jnp.concatenate([lo, hi], axis=1)

    for ref, pad in ((a1p, 16), (g2p, 16), (g3p, 32)):
        clear_edges(ref, pad)

    state = []
    for a in range(GROUPS):
        rows = slice(HEIGHT * a, HEIGHT * (a + 1))
        a0_ref[0, rows, :] = block(a)
        raw = block(3 + a)
        state.append(raw)
        a0_ref[1, rows, :] = gelu(raw.astype(F32)).astype(BF16)
        a0_ref[2, rows, :] = block(6 + a)
        cot = block(9 + a)
        g3_ref[rows, :] = cot
        g3p[a, 32 : 32 + HEIGHT, :] = cot

    sums = []
    for i in range(3):
        total = None
        for j in range(3):
            term = dot(a0_ref[j], w_ref[3 * i + j])
            total = term if total is None else total + term
        sums.append(total)
    for a in range(GROUPS):
        rows = slice(HEIGHT * a, HEIGHT * (a + 1))
        branch = shifted_rows(sums[0][rows], -1) + sums[1][rows] + shifted_rows(sums[2][rows], 1)
        state[a] = (state[a].astype(F32) + branch).astype(BF16)
        act, slope = gelu_and_slope(state[a].astype(F32))
        act = act.astype(BF16)
        slope1[rows, :] = slope
        a1_ref[rows, :] = act
        a1p[a, 16 : 16 + HEIGHT, :] = act

    branch = spread_conv(a1p, w_ref, 1, 16, 1, False)
    for a in range(GROUPS):
        rows = slice(HEIGHT * a, HEIGHT * (a + 1))
        state[a] = (state[a].astype(F32) + branch[a]).astype(BF16)
        act, slope = gelu_and_slope(state[a].astype(F32))
        act = act.astype(BF16)
        slope2[rows, :] = slope
        a2_ref[rows, :] = act
        s2_ref[rows, :] = state[a]

    back = spread_conv(g3p, w_ref, 2, 32, 2, True)
    for a in range(GROUPS):
        rows = slice(HEIGHT * a, HEIGHT * (a + 1))
        grad = g3_ref[rows, :].astype(F32) + back[a] * slope2[rows, :]
        grad = grad.astype(BF16)
        g2_ref[rows, :] = grad
        g2p[a, 16 : 16 + HEIGHT, :] = grad

    back = spread_conv(g2p, w_ref, 1, 16, 1, True)
    for a in range(GROUPS):
        rows = slice(HEIGHT * a, HEIGHT * (a + 1))
        grad = g2_ref[rows, :].astype(F32) + back[a] * slope1[rows, :]
        g1_ref[rows, :] = grad.astype(BF16)


def final_kernel(a2_ref, s2_ref, g1_ref, w_ref, send_ref, a2p):
    clear_edges(a2p, 32)
    for a in range(GROUPS):
        a2p[a, 32 : 32 + HEIGHT, :] = a2_ref[HEIGHT * a : HEIGHT * (a + 1), :]
    branch = spread_conv(a2p, w_ref, 2, 32, 2, False)
    state, grads = [], []
    for a in range(GROUPS):
        rows = slice(HEIGHT * a, HEIGHT * (a + 1))
        state.append(s2_ref[rows, :].astype(F32) + branch[a])
        grads.append(g1_ref[rows, :].astype(F32))

    blocks = grads + state
    for k in range(6):
        send_ref[:, 16 * k : 16 * k + 16, :] = blocks[k][:, 0:128].astype(BF16).reshape(16, 16, 128)
    for k in range(3):
        both = jnp.concatenate([blocks[2 * k][:, 128:192], blocks[2 * k + 1][:, 128:192]], axis=1)
        send_ref[:, 96 + 16 * k : 112 + 16 * k, :] = both.astype(BF16).reshape(16, 16, 128)
    third = jnp.concatenate([grads[2][:, 128:192], jnp.zeros((HEIGHT, 64), F32)], axis=1)
    first = jnp.concatenate([grads[0][:, 128:192], grads[1][:, 128:192]], axis=1)
    parts = [grads[0][:, 0:128], grads[1][:, 0:128], grads[2][:, 0:128], first, third]
    index = lax.broadcasted_iota(jnp.int32, (HEIGHT, 128), 0)
    inner = index % 16
    halo = jnp.zeros((HEIGHT, 128), F32)
    for n, part in enumerate(parts):
        p = 2 * n
        above = pltpu.roll(part, p + 1, 0)
        halo = jnp.where((inner == p) & (index >= 16), above, halo)
        p = 2 * n + 1
        below = pltpu.roll(part, (HEIGHT + p - 16) % HEIGHT, 0)
        halo = jnp.where((inner == p) & (index < HEIGHT - 16), below, halo)
    send_ref[:, 144:160, :] = halo.astype(BF16).reshape(16, 16, 128)


def wgrad_kernel(a0_ref, a1_ref, a2_ref, g1_ref, g2_ref, g3_ref, order_ref, keep_ref, give_ref, gp, acts):
    order = order_ref[...]

    def store(tap, value):
        keep_ref[tap] = value[0:96, :].astype(BF16)
        give_ref[tap] = value[96:192, :].astype(BF16)

    def spread_grad(layer, act_ref, grad_ref, width, step):
        for a in range(GROUPS):
            gp[a, 0:width, :] = jnp.zeros((width, CH), BF16)
            gp[a, width : width + HEIGHT, :] = grad_ref[HEIGHT * a : HEIGHT * (a + 1), :]
            gp[a, width + HEIGHT : 2 * width + HEIGHT, :] = jnp.zeros((width, CH), BF16)
        acts[...] = dot_t(order, act_ref[...]).astype(BF16)
        for j in range(3):
            off = (1 - j) * step
            sources = [a for a in range(GROUPS) if 0 <= a + off < GROUPS]
            lo, n = sources[0], len(sources)
            left = acts[:, HEIGHT * lo : HEIGHT * (lo + n)]
            for i in range(3):
                at = width * (2 - i)
                right = gp[lo + off : lo + off + n, at : at + HEIGHT, :].reshape(n * HEIGHT, CH)
                store(9 * layer + 3 * i + j, dot(left, right))

    spread_grad(2, a2_ref, g3_ref, 32, 2)
    spread_grad(1, a1_ref, g2_ref, 16, 1)
    shifted = [[], g1_ref[...], []]
    for a in range(GROUPS):
        rows = g1_ref[HEIGHT * a : HEIGHT * (a + 1), :].astype(F32)
        shifted[0].append(shifted_rows(rows, 1).astype(BF16))
        shifted[2].append(shifted_rows(rows, -1).astype(BF16))
    shifted[0] = jnp.concatenate(shifted[0], axis=0)
    shifted[2] = jnp.concatenate(shifted[2], axis=0)
    for j in range(3):
        acts[...] = dot_t(order, a0_ref[j]).astype(BF16)
        for i in range(3):
            store(3 * i + j, dot(acts[...], shifted[i]))


PIECES = (
    ((0, 0, 72),),
    ((0, 72, 144),),
    ((0, 144, 192), (1, 0, 24)),
    ((1, 24, 96),),
    ((1, 96, 168),),
    ((1, 168, 192), (2, 0, 48)),
    ((2, 48, 120),),
    ((2, 120, 192),),
)


def split_kernel(keep_ref, got_ref, part_ref, send_ref):
    send_ref[:, 256:416, :] = part_ref[...]
    total = (keep_ref[...].astype(F32) + got_ref[...].astype(F32)).astype(BF16)
    for h in range(2):
        for t, pieces in enumerate(PIECES):
            for group in range(4):
                parts = []
                for tap in range(7 * group, min(7 * group + 7, 27)):
                    for j, lo, hi in pieces:
                        at = 48 * h + 16 * j
                        parts.append(total[tap, at : at + 16, lo:hi])
                parts.append(jnp.zeros((16, 80 if group == 3 else 8), BF16))
                line = jnp.concatenate(parts, axis=1)
                for n in range(4):
                    at = 64 * group + 16 * n
                    send_ref[8 * h + t, at : at + 16, :] = line[:, 128 * n : 128 * n + 128]


def gather_kernel(got_ref, send_ref, total_ref):
    total = got_ref[0, 0:256, :].astype(F32)
    for s in range(1, 16):
        total = total + got_ref[s, 0:256, :].astype(F32)
    total_ref[...] = total
    for z in range(16):
        send_ref[z] = total_ref[pl.ds(z, 16, stride=16), :].astype(BF16)


def finish_kernel(scale, got_ref, out_ref):
    total = got_ref[0].astype(F32)
    for z in range(1, 16):
        total = total + got_ref[z].astype(F32)
    total = total * scale
    for tap in range(27):
        start = 512 * (tap // 7) + 72 * (tap % 7)
        parts = []
        while sum(part.shape[1] for part in parts) < 72:
            at = start + sum(part.shape[1] for part in parts)
            end = min(start + 72, (at // 128 + 1) * 128)
            row = at // 128
            parts.append(total[row : row + 1, at % 128 : at % 128 + end - at])
        out_ref[tap : tap + 1, :] = parts[0] if len(parts) == 1 else jnp.concatenate(parts, axis=1)


def last_kernel(recv_ref, x_ref, w_ref, out_ref, grad_ref, padded, slope_ref, grads_ref):
    def tile(k):
        at = 256 + 16 * k
        return recv_ref[:, at : at + 16, :].reshape(HEIGHT, 128).astype(F32)

    lows = [tile(k) for k in range(6)]
    highs = []
    for k in range(3):
        both = tile(6 + k)
        highs += [both[:, 0:64], both[:, 64:128]]
    halo = tile(9)
    inner = lax.broadcasted_iota(jnp.int32, (HEIGHT, CH), 0) % 16

    def pair(left, right):
        return jnp.concatenate([left, right], axis=1)

    final = [jnp.concatenate([lows[3 + a], highs[3 + a]], axis=1) for a in range(GROUPS)]
    for p in range(WIDTH // 2):
        a, b = (2 * p) // 16, (2 * p) % 16
        left = final[a][16 * b : 16 * b + 16]
        right = final[a][16 * b + 16 : 16 * b + 32]
        out_ref[0, :, 384 * p : 384 * p + 384] = pair(left, right).astype(BF16)

    zeros = jnp.zeros((16, CH), BF16)
    for i in range(3):
        padded[i, 0:16, :] = zeros
        padded[i, 16 + CELLS : 32 + CELLS, :] = zeros
    for a in range(GROUPS):
        at = 16 + HEIGHT * a
        here = jnp.concatenate([lows[a], highs[a]], axis=1)
        grads_ref[HEIGHT * a : HEIGHT * (a + 1), :] = here

        def edge(row, p_lo, p_hi, lane):
            low = pltpu.roll(halo, (row - p_lo) % HEIGHT, 0)
            high = pltpu.roll(halo, (row - p_hi) % HEIGHT, 0)[:, lane : lane + 64]
            return jnp.concatenate([low, high], axis=1)

        hi_slot, lane = ((6, 0), (6, 64), (8, 0))[a]
        above = edge(0, 2 * a, hi_slot, lane)
        below = edge(15, 2 * a + 1, hi_slot + 1, lane)
        after = jnp.where(inner == 15, below, pltpu.roll(here, HEIGHT - 1, 0))
        before = jnp.where(inner == 0, above, pltpu.roll(here, 1, 0))
        padded[0, at : at + HEIGHT, :] = after.astype(BF16)
        padded[1, at : at + HEIGHT, :] = here.astype(BF16)
        padded[2, at : at + HEIGHT, :] = before.astype(BF16)

    for p in range(WIDTH // 2):
        values = x_ref[0, :, 384 * p : 384 * p + 384].astype(F32)
        slope = gelu_and_slope(values)[1]
        slope_ref[32 * p : 32 * p + 16, :] = slope[:, 0:192]
        slope_ref[32 * p + 16 : 32 * p + 32, :] = slope[:, 192:384]

    total = None
    for i in range(3):
        for j in range(3):
            at = 16 * (2 - j)
            term = dot_t(padded[i, at : at + CELLS, :], w_ref[3 * i + j])
            total = term if total is None else total + term
    result = grads_ref[...] + total * slope_ref[...]
    for p in range(WIDTH // 2):
        left = result[32 * p : 32 * p + 16]
        right = result[32 * p + 16 : 32 * p + 32]
        grad_ref[0, :, 384 * p : 384 * p + 384] = pair(left, right).astype(BF16)


def body(inputs, cotangent, weights):
    count = math.prod(lax.axis_size(axis) for axis in DP + SPACE)
    scale = 1.0 / math.sqrt(count * ROWS * WIDTH)
    core = lax.axis_index("core")

    place = jnp.arange(CH)
    half = (core + place // 96) % 2
    channel = 12 * (place % 16) + 6 * half + 3 * ((place // 48) % 2) + (place // 16) % 3
    order = (channel[:, None] == jnp.arange(CH)[None, :]).astype(BF16)

    send = call(
        pack_kernel,
        shape(16, 288, 128),
        after=(inputs, cotangent),
        scratch=(
            pltpu.VMEM((1, ROWS, 9216), BF16),
            pltpu.VMEM((1, ROWS, 9216), BF16),
            pltpu.VMEM((ROWS, 9216), BF16),
            pltpu.SemaphoreType.DMA((2,)),
        ),
        moved=2500000,
    )
    recv = lax.all_to_all(send, SPACE, 0, 0, tiled=True)
    kernels = weights.reshape(27, CH, CH)
    a0, a1, a2, g1, g2, g3, s2 = call(
        main_kernel,
        (shape(3, CELLS, CH),) + (shape(CELLS, CH),) * 6,
        recv,
        kernels,
        scratch=(
            pltpu.VMEM((GROUPS, HEIGHT + 32, CH), BF16),
            pltpu.VMEM((GROUPS, HEIGHT + 32, CH), BF16),
            pltpu.VMEM((GROUPS, HEIGHT + 64, CH), BF16),
            pltpu.VMEM((CELLS, CH), F32),
            pltpu.VMEM((CELLS, CH), F32),
        ),
        flops=4 * 2 * CELLS * 9 * CH * CH,
        moved=9000000,
    )
    keep, give = call(
        wgrad_kernel,
        (shape(27, 96, CH), shape(27, 96, CH)),
        a0, a1, a2, g1, g2, g3, order,
        scratch=(pltpu.VMEM((GROUPS, HEIGHT + 64, CH), BF16), pltpu.VMEM((CH, CELLS), BF16)),
        flops=3 * 2 * CELLS * 9 * CH * CH,
        moved=7000000,
    )
    got = lax.ppermute(give, "core", [(0, 1), (1, 0)])
    part = call(
        final_kernel,
        shape(16, 160, 128),
        a2, s2, g1, kernels,
        scratch=(pltpu.VMEM((GROUPS, HEIGHT + 64, CH), BF16),),
        flops=2 * CELLS * 9 * CH * CH,
        moved=4500000,
    )
    send = call(split_kernel, shape(16, 416, 128), keep, got, part, moved=5000000)
    back = lax.all_to_all(send, SPACE, 0, 0, tiled=True)
    send, _ = call(
        gather_kernel, (shape(16, 16, 128), shape(256, 128, dtype=F32)), back, moved=2000000
    )
    got = lax.all_to_all(send, "z", 0, 0, tiled=True)
    weight_grad = call(
        lambda *refs: finish_kernel(scale, *refs), shape(27, 72, dtype=F32), got, moved=150000
    )
    outputs, input_grad = call(
        last_kernel,
        (shape(1, ROWS, 9216), shape(1, ROWS, 9216)),
        back, inputs, kernels,
        scratch=(
            pltpu.VMEM((3, CELLS + 32, CH), BF16),
            pltpu.VMEM((CELLS, CH), F32),
            pltpu.VMEM((CELLS, CH), F32),
        ),
        flops=2 * CELLS * 9 * CH * CH,
        moved=3000000,
    )
    return outputs, input_grad, weight_grad


def solution(mesh):
    devices = mesh.devices.reshape(16, 2, 4, 4)
    wide = Mesh(devices, DP + SPACE)
    placed = (P(DP, SPACE, None), P(DP, SPACE, None), P())
    return jax.shard_map(
        body,
        mesh=wide,
        in_specs=placed,
        out_specs=(P(DP, SPACE, None), P(DP, SPACE, None), P(None, DP + SPACE)),
        check_vma=False,
    )
```

```python
import math

import jax
import jax.numpy as jnp
from jax import lax
from jax.experimental import pallas as pl
from jax.experimental.pallas import tpu as pltpu
from jax.sharding import Mesh
from jax.sharding import PartitionSpec as P


DP = ("z", "core")
SPACE = ("x", "y")
CH = 192
ROWS = 16
WIDTH = 48
HEIGHT = 256
GROUPS = 3
CELLS = GROUPS * HEIGHT
F32 = jnp.float32
BF16 = jnp.bfloat16
GELU_A = math.sqrt(2.0 / math.pi)
GELU_B = 0.044715
VMEM_LIMIT = 24 * 1024 * 1024
VMEM_MOST = 60 * 1024 * 1024


def gelu(x):
    return x * (0.5 * (1.0 + jnp.tanh(GELU_A * (x + GELU_B * (x * x * x)))))


def gelu_and_slope(x):
    square = x * x
    tanh = jnp.tanh(GELU_A * (x + GELU_B * (x * square)))
    cdf = 0.5 * (1.0 + tanh)
    slope = cdf + (0.5 * x) * ((1.0 - tanh * tanh) * (GELU_A + (3.0 * GELU_A * GELU_B) * square))
    return x * cdf, slope


def dot(a, b):
    return lax.dot_general(a, b, (((1,), (0,)), ((), ())), preferred_element_type=F32)


def dot_t(a, b):
    return lax.dot_general(a, b, (((1,), (1,)), ((), ())), preferred_element_type=F32)


def call(kernel, out_shape, *args, scratch=(), flops=0, moved=0, remain=(), limit=VMEM_LIMIT, apart=0):
    outputs = jax.tree.leaves(out_shape)
    spaces = [pltpu.VMEM] * (len(outputs) - apart) + [pltpu.HBM] * apart
    specs = [pl.BlockSpec(memory_space=space) for space in spaces]
    return pl.pallas_call(
        kernel,
        out_shape=out_shape,
        in_specs=[pl.BlockSpec(memory_space=pltpu.HBM)] * len(remain)
        + [pl.BlockSpec(memory_space=pltpu.VMEM)] * len(args),
        out_specs=jax.tree.unflatten(jax.tree.structure(out_shape), specs),
        scratch_shapes=list(scratch),
        compiler_params=pltpu.CompilerParams(vmem_limit_bytes=limit),
        cost_estimate=pl.CostEstimate(flops=flops, bytes_accessed=moved, transcendentals=0),
    )(*remain, *args)


def shape(*dims, dtype=BF16):
    return jax.ShapeDtypeStruct(dims, dtype)


def pack_kernel(x_hbm, c_hbm, send_hbm, x_ref, c_ref, act_ref, send_ref, sems, send_sems):
    copies = [
        pltpu.make_async_copy(x_hbm, x_ref, sems.at[0]),
        pltpu.make_async_copy(c_hbm, c_ref, sems.at[1]),
    ]
    for copy in copies:
        copy.start()
    for copy in copies:
        copy.wait()
    act_ref[...] = gelu(x_ref[0].astype(F32)).astype(BF16)

    def column(load, w):
        pair = load(384 * (w // 2))
        base = 192 * (w % 2)
        return pair[:, base : base + 128], pair[:, base + 128 : base + 192]

    nothing = jnp.zeros((16, 128), BF16), jnp.zeros((16, 64), BF16)
    act, raw, cot, leaving = [], [], [], []
    for w in range(WIDTH):
        act.append(column(lambda at: act_ref[:, at : at + 384], w))
        raw.append(column(lambda at: x_ref[0, :, at : at + 384], w))
        cot.append(column(lambda at: c_ref[0, :, at : at + 384], w))
    for b in range(16):
        blocks = []
        for g in range(4):
            for a in range(GROUPS):
                w = 16 * a + b
                if g == 0:
                    blocks.append(act[w - 1] if w > 0 else nothing)
                elif g == 1:
                    blocks.append(raw[w])
                elif g == 2:
                    blocks.append(act[w + 1] if w < WIDTH - 1 else nothing)
                else:
                    blocks.append(cot[w])
        for k in range(12):
            send_ref[b, 16 * k : 16 * k + 16, :] = blocks[k][0]
        for k in range(6):
            both = jnp.concatenate([blocks[2 * k][1], blocks[2 * k + 1][1]], axis=1)
            send_ref[b, 192 + 16 * k : 208 + 16 * k, :] = both
        leaving.append(pltpu.make_async_copy(send_ref.at[b], send_hbm.at[b], send_sems.at[b]))
        leaving[b].start()
    for copy in leaving:
        copy.wait()


def shifted_rows(value, by):
    rows = lax.broadcasted_iota(jnp.int32, value.shape, 0)
    rolled = pltpu.roll(value, (-by) % value.shape[0], 0)
    keep = rows != (0 if by < 0 else value.shape[0] - 1)
    return jnp.where(keep, rolled, 0.0)


def spread_conv(padded, w_ref, layer, width, step, transposed):
    totals = []
    for a in range(GROUPS):
        cells, taps = [], []
        for j in range(3):
            src = a + ((1 - j) * step if transposed else (j - 1) * step)
            if not 0 <= src < GROUPS:
                continue
            for i in range(3):
                at = width * (2 - i) if transposed else width * i
                cells.append(padded[src, at : at + HEIGHT, :])
                taps.append(w_ref[9 * layer + 3 * i + j])
        cells = jnp.concatenate(cells, axis=1)
        if transposed:
            totals.append(dot_t(cells, jnp.concatenate(taps, axis=1)))
        else:
            totals.append(dot(cells, jnp.concatenate(taps, axis=0)))
    return totals


def clear_edges(ref, pad):
    for a in range(GROUPS):
        ref[a, 0:pad, :] = jnp.zeros((pad, CH), BF16)
        ref[a, pad + HEIGHT : 2 * pad + HEIGHT, :] = jnp.zeros((pad, CH), BF16)


MAIN_SCRATCH = (
    pltpu.VMEM((16, 288, 128), BF16),
    pltpu.VMEM((CELLS, 3 * CH), BF16),
    pltpu.VMEM((GROUPS, HEIGHT + 32, CH), BF16),
    pltpu.VMEM((GROUPS, HEIGHT + 32, CH), BF16),
    pltpu.VMEM((GROUPS, HEIGHT + 64, CH), BF16),
    pltpu.VMEM((CELLS, CH), F32),
    pltpu.VMEM((CELLS, CH), F32),
    pltpu.SemaphoreType.DMA((3,)),
)


def main_kernel(
    recv_hbm, w_ref, a0_ref, a1_ref, a2_ref, g1_ref, g2_ref, g3_ref, s2_ref,
    recv_ref, a0p, a1p, g2p, g3p, slope1, slope2, sems,
):
    def rows_copy(n, lo, hi):
        part = pltpu.make_async_copy(
            recv_hbm.at[:, lo:hi, :], recv_ref.at[:, lo:hi, :], sems.at[n]
        )
        part.start()
        return part

    moving = [rows_copy(0, 0, 144), rows_copy(1, 192, 288), rows_copy(2, 144, 192)]

    def block(k):
        lo = recv_ref[:, 16 * k : 16 * k + 16, :].reshape(HEIGHT, 128)
        at = 192 + 16 * (k // 2)
        hi = recv_ref[:, at : at + 16, :].reshape(HEIGHT, 128)[:, 64 * (k % 2) : 64 * (k % 2) + 64]
        return jnp.concatenate([lo, hi], axis=1)

    for ref, pad in ((a1p, 16), (g2p, 16), (g3p, 32)):
        clear_edges(ref, pad)

    moving[0].wait()
    moving[1].wait()
    state = []
    for a in range(GROUPS):
        rows = slice(HEIGHT * a, HEIGHT * (a + 1))
        raw = block(3 + a)
        state.append(raw)
        for j in range(3):
            value = gelu(raw.astype(F32)).astype(BF16) if j == 1 else block(3 * j + a)
            a0_ref[j, rows, :] = value
            a0p[rows, CH * j : CH * (j + 1)] = value

    sums = [[], [], []]
    for a in range(GROUPS):
        rows = slice(HEIGHT * a, HEIGHT * (a + 1))
        for i in range(3):
            taps = jnp.concatenate([w_ref[3 * i + j] for j in range(3)], axis=0)
            sums[i].append(dot(a0p[rows, :], taps))
    moving[2].wait()
    for a in range(GROUPS):
        cot = block(9 + a)
        g3_ref[HEIGHT * a : HEIGHT * (a + 1), :] = cot
        g3p[a, 32 : 32 + HEIGHT, :] = cot
    back = spread_conv(g3p, w_ref, 2, 32, 2, True)
    for a in range(GROUPS):
        rows = slice(HEIGHT * a, HEIGHT * (a + 1))
        branch = shifted_rows(sums[0][a], -1) + sums[1][a] + shifted_rows(sums[2][a], 1)
        state[a] = (state[a].astype(F32) + branch).astype(BF16)
        act, slope = gelu_and_slope(state[a].astype(F32))
        act = act.astype(BF16)
        slope1[rows, :] = slope
        a1_ref[rows, :] = act
        a1p[a, 16 : 16 + HEIGHT, :] = act

    branch = spread_conv(a1p, w_ref, 1, 16, 1, False)
    for a in range(GROUPS):
        rows = slice(HEIGHT * a, HEIGHT * (a + 1))
        state[a] = (state[a].astype(F32) + branch[a]).astype(BF16)
        act, slope = gelu_and_slope(state[a].astype(F32))
        act = act.astype(BF16)
        slope2[rows, :] = slope
        a2_ref[rows, :] = act
        s2_ref[rows, :] = state[a]

    for a in range(GROUPS):
        rows = slice(HEIGHT * a, HEIGHT * (a + 1))
        grad = g3_ref[rows, :].astype(F32) + back[a] * slope2[rows, :]
        grad = grad.astype(BF16)
        g2_ref[rows, :] = grad
        g2p[a, 16 : 16 + HEIGHT, :] = grad

    back = spread_conv(g2p, w_ref, 1, 16, 1, True)
    for a in range(GROUPS):
        rows = slice(HEIGHT * a, HEIGHT * (a + 1))
        grad = g2_ref[rows, :].astype(F32) + back[a] * slope1[rows, :]
        g1_ref[rows, :] = grad.astype(BF16)


def final_kernel(a2_ref, s2_ref, g1_ref, w_ref, send_ref, a2p):
    clear_edges(a2p, 32)
    for a in range(GROUPS):
        a2p[a, 32 : 32 + HEIGHT, :] = a2_ref[HEIGHT * a : HEIGHT * (a + 1), :]
    branch = spread_conv(a2p, w_ref, 2, 32, 2, False)
    state, grads = [], []
    for a in range(GROUPS):
        rows = slice(HEIGHT * a, HEIGHT * (a + 1))
        state.append(s2_ref[rows, :].astype(F32) + branch[a])
        grads.append(g1_ref[rows, :].astype(F32))

    blocks = grads + state
    for k in range(6):
        send_ref[:, 16 * k : 16 * k + 16, :] = blocks[k][:, 0:128].astype(BF16).reshape(16, 16, 128)
    for k in range(3):
        both = jnp.concatenate([blocks[2 * k][:, 128:192], blocks[2 * k + 1][:, 128:192]], axis=1)
        send_ref[:, 96 + 16 * k : 112 + 16 * k, :] = both.astype(BF16).reshape(16, 16, 128)
    third = jnp.concatenate([grads[2][:, 128:192], jnp.zeros((HEIGHT, 64), F32)], axis=1)
    first = jnp.concatenate([grads[0][:, 128:192], grads[1][:, 128:192]], axis=1)
    parts = [grads[0][:, 0:128], grads[1][:, 0:128], grads[2][:, 0:128], first, third]
    index = lax.broadcasted_iota(jnp.int32, (HEIGHT, 128), 0)
    inner = index % 16
    halo = jnp.zeros((HEIGHT, 128), F32)
    for n, part in enumerate(parts):
        p = 2 * n
        above = pltpu.roll(part, p + 1, 0)
        halo = jnp.where((inner == p) & (index >= 16), above, halo)
        p = 2 * n + 1
        below = pltpu.roll(part, (HEIGHT + p - 16) % HEIGHT, 0)
        halo = jnp.where((inner == p) & (index < HEIGHT - 16), below, halo)
    send_ref[:, 144:160, :] = halo.astype(BF16).reshape(16, 16, 128)


def wgrad_kernel(a0_ref, a1_ref, a2_ref, g1_ref, g2_ref, g3_ref, order_ref, keep_ref, give_ref, gp, acts):
    order = order_ref[...]

    def store(tap, value):
        keep_ref[tap] = value[0:96, :].astype(BF16)
        give_ref[tap] = value[96:192, :].astype(BF16)

    def spread_grad(layer, act_ref, grad_ref, width, step):
        for a in range(GROUPS):
            gp[a, 0:width, :] = jnp.zeros((width, CH), BF16)
            gp[a, width : width + HEIGHT, :] = grad_ref[HEIGHT * a : HEIGHT * (a + 1), :]
            gp[a, width + HEIGHT : 2 * width + HEIGHT, :] = jnp.zeros((width, CH), BF16)
        acts[...] = dot_t(order, act_ref[...]).astype(BF16)
        for j in range(3):
            off = (1 - j) * step
            sources = [a for a in range(GROUPS) if 0 <= a + off < GROUPS]
            lo, n = sources[0], len(sources)
            left = acts[:, HEIGHT * lo : HEIGHT * (lo + n)]
            for i in range(3):
                at = width * (2 - i)
                right = gp[lo + off : lo + off + n, at : at + HEIGHT, :].reshape(n * HEIGHT, CH)
                store(9 * layer + 3 * i + j, dot(left, right))

    spread_grad(2, a2_ref, g3_ref, 32, 2)
    spread_grad(1, a1_ref, g2_ref, 16, 1)
    shifted = [[], g1_ref[...], []]
    for a in range(GROUPS):
        rows = g1_ref[HEIGHT * a : HEIGHT * (a + 1), :].astype(F32)
        shifted[0].append(shifted_rows(rows, 1).astype(BF16))
        shifted[2].append(shifted_rows(rows, -1).astype(BF16))
    shifted[0] = jnp.concatenate(shifted[0], axis=0)
    shifted[2] = jnp.concatenate(shifted[2], axis=0)
    for j in range(3):
        acts[...] = dot_t(order, a0_ref[j]).astype(BF16)
        for i in range(3):
            store(3 * i + j, dot(acts[...], shifted[i]))


PIECES = (
    ((0, 0, 72),),
    ((0, 72, 144),),
    ((0, 144, 192), (1, 0, 24)),
    ((1, 24, 96),),
    ((1, 96, 168),),
    ((1, 168, 192), (2, 0, 48)),
    ((2, 48, 120),),
    ((2, 120, 192),),
)


def split_kernel(keep_ref, got_ref, part_ref, send_ref):
    send_ref[:, 256:416, :] = part_ref[...]
    total = (keep_ref[...].astype(F32) + got_ref[...].astype(F32)).astype(BF16)
    for h in range(2):
        for t, pieces in enumerate(PIECES):
            for group in range(4):
                parts = []
                for tap in range(7 * group, min(7 * group + 7, 27)):
                    for j, lo, hi in pieces:
                        at = 48 * h + 16 * j
                        parts.append(total[tap, at : at + 16, lo:hi])
                parts.append(jnp.zeros((16, 80 if group == 3 else 8), BF16))
                line = jnp.concatenate(parts, axis=1)
                for n in range(4):
                    at = 64 * group + 16 * n
                    send_ref[8 * h + t, at : at + 16, :] = line[:, 128 * n : 128 * n + 128]


def gather_kernel(got_ref, send_ref, rest_hbm, total_ref, sem):
    rest = pltpu.make_async_copy(got_ref.at[:, 256:416, :], rest_hbm, sem)
    rest.start()
    total = got_ref[0, 0:256, :].astype(F32)
    for s in range(1, 16):
        total = total + got_ref[s, 0:256, :].astype(F32)
    total_ref[...] = total
    for z in range(16):
        send_ref[z] = total_ref[pl.ds(z, 16, stride=16), :].astype(BF16)
    rest.wait()


def finish_kernel(scale, got_ref, out_ref):
    total = got_ref[0].astype(F32)
    for z in range(1, 16):
        total = total + got_ref[z].astype(F32)
    total = total * scale
    for tap in range(27):
        start = 512 * (tap // 7) + 72 * (tap % 7)
        parts = []
        while sum(part.shape[1] for part in parts) < 72:
            at = start + sum(part.shape[1] for part in parts)
            end = min(start + 72, (at // 128 + 1) * 128)
            row = at // 128
            parts.append(total[row : row + 1, at % 128 : at % 128 + end - at])
        out_ref[tap : tap + 1, :] = parts[0] if len(parts) == 1 else jnp.concatenate(parts, axis=1)


def last_kernel(recv_ref, x_ref, w_ref, out_ref, grad_ref, padded, slope_ref, grads_ref):
    def tile(k):
        return recv_ref[:, 16 * k : 16 * k + 16, :].reshape(HEIGHT, 128).astype(F32)

    lows = [tile(k) for k in range(6)]
    highs = []
    for k in range(3):
        both = tile(6 + k)
        highs += [both[:, 0:64], both[:, 64:128]]
    halo = tile(9)
    inner = lax.broadcasted_iota(jnp.int32, (HEIGHT, CH), 0) % 16

    def pair(left, right):
        return jnp.concatenate([left, right], axis=1)

    final = [jnp.concatenate([lows[3 + a], highs[3 + a]], axis=1) for a in range(GROUPS)]
    for p in range(WIDTH // 2):
        a, b = (2 * p) // 16, (2 * p) % 16
        left = final[a][16 * b : 16 * b + 16]
        right = final[a][16 * b + 16 : 16 * b + 32]
        out_ref[0, :, 384 * p : 384 * p + 384] = pair(left, right).astype(BF16)

    zeros = jnp.zeros((16, CH), BF16)
    for i in range(3):
        padded[i, 0:16, :] = zeros
        padded[i, 16 + CELLS : 32 + CELLS, :] = zeros
    for a in range(GROUPS):
        at = 16 + HEIGHT * a
        here = jnp.concatenate([lows[a], highs[a]], axis=1)
        grads_ref[HEIGHT * a : HEIGHT * (a + 1), :] = here

        def edge(row, p_lo, p_hi, lane):
            low = pltpu.roll(halo, (row - p_lo) % HEIGHT, 0)
            high = pltpu.roll(halo, (row - p_hi) % HEIGHT, 0)[:, lane : lane + 64]
            return jnp.concatenate([low, high], axis=1)

        hi_slot, lane = ((6, 0), (6, 64), (8, 0))[a]
        above = edge(0, 2 * a, hi_slot, lane)
        below = edge(15, 2 * a + 1, hi_slot + 1, lane)
        after = jnp.where(inner == 15, below, pltpu.roll(here, HEIGHT - 1, 0))
        before = jnp.where(inner == 0, above, pltpu.roll(here, 1, 0))
        padded[0, at : at + HEIGHT, :] = after.astype(BF16)
        padded[1, at : at + HEIGHT, :] = here.astype(BF16)
        padded[2, at : at + HEIGHT, :] = before.astype(BF16)

    for p in range(WIDTH // 2):
        values = x_ref[0, :, 384 * p : 384 * p + 384].astype(F32)
        slope = gelu_and_slope(values)[1]
        slope_ref[32 * p : 32 * p + 16, :] = slope[:, 0:192]
        slope_ref[32 * p + 16 : 32 * p + 32, :] = slope[:, 192:384]

    cells, taps = [], []
    for i in range(3):
        for j in range(3):
            at = 16 * (2 - j)
            cells.append(padded[i, at : at + CELLS, :])
            taps.append(w_ref[3 * i + j])
    total = dot_t(jnp.concatenate(cells, axis=1), jnp.concatenate(taps, axis=1))
    result = grads_ref[...] + total * slope_ref[...]
    for p in range(WIDTH // 2):
        left = result[32 * p : 32 * p + 16]
        right = result[32 * p + 16 : 32 * p + 32]
        grad_ref[0, :, 384 * p : 384 * p + 384] = pair(left, right).astype(BF16)


def body(inputs, cotangent, weights):
    count = math.prod(lax.axis_size(axis) for axis in DP + SPACE)
    scale = 1.0 / math.sqrt(count * ROWS * WIDTH)
    core = lax.axis_index("core")

    place = jnp.arange(CH)
    half = (core + place // 96) % 2
    channel = 12 * (place % 16) + 6 * half + 3 * ((place // 48) % 2) + (place // 16) % 3
    order = (channel[:, None] == jnp.arange(CH)[None, :]).astype(BF16)

    send = call(
        pack_kernel,
        shape(16, 288, 128),
        remain=(inputs, cotangent),
        scratch=(
            pltpu.VMEM((1, ROWS, 9216), BF16),
            pltpu.VMEM((1, ROWS, 9216), BF16),
            pltpu.VMEM((ROWS, 9216), BF16),
            pltpu.VMEM((16, 288, 128), BF16),
            pltpu.SemaphoreType.DMA((2,)),
            pltpu.SemaphoreType.DMA((16,)),
        ),
        moved=2500000,
        apart=1,
        limit=VMEM_MOST,
    )
    recv = lax.all_to_all(send, SPACE, 0, 0, tiled=True)
    kernels = weights.reshape(27, CH, CH)
    a0, a1, a2, g1, g2, g3, s2 = call(
        main_kernel,
        (shape(3, CELLS, CH),) + (shape(CELLS, CH),) * 6,
        kernels,
        remain=(recv,),
        scratch=MAIN_SCRATCH,
        flops=4 * 2 * CELLS * 9 * CH * CH,
        moved=9000000,
    )
    keep, give = call(
        wgrad_kernel,
        (shape(27, 96, CH), shape(27, 96, CH)),
        a0, a1, a2, g1, g2, g3, order,
        scratch=(pltpu.VMEM((GROUPS, HEIGHT + 64, CH), BF16), pltpu.VMEM((CH, CELLS), BF16)),
        flops=3 * 2 * CELLS * 9 * CH * CH,
        moved=7000000,
    )
    got = lax.ppermute(give, "core", [(0, 1), (1, 0)])
    part = call(
        final_kernel,
        shape(16, 160, 128),
        a2, s2, g1, kernels,
        scratch=(pltpu.VMEM((GROUPS, HEIGHT + 64, CH), BF16),),
        flops=2 * CELLS * 9 * CH * CH,
        moved=4500000,
    )
    send = call(split_kernel, shape(16, 416, 128), keep, got, part, moved=5000000)
    back = lax.all_to_all(send, SPACE, 0, 0, tiled=True)
    send, rest = call(
        gather_kernel,
        (shape(16, 16, 128), shape(16, 160, 128)),
        back,
        scratch=(pltpu.VMEM((256, 128), F32), pltpu.SemaphoreType.DMA),
        moved=2500000,
        apart=1,
    )
    got = lax.all_to_all(send, "z", 0, 0, tiled=True)
    weight_grad = call(
        lambda *refs: finish_kernel(scale, *refs), shape(27, 72, dtype=F32), got, moved=150000
    )
    outputs, input_grad = call(
        last_kernel,
        (shape(1, ROWS, 9216), shape(1, ROWS, 9216)),
        rest, inputs, kernels,
        scratch=(
            pltpu.VMEM((3, CELLS + 32, CH), BF16),
            pltpu.VMEM((CELLS, CH), F32),
            pltpu.VMEM((CELLS, CH), F32),
        ),
        flops=2 * CELLS * 9 * CH * CH,
        moved=3000000,
    )
    return outputs, input_grad, weight_grad


def solution(mesh):
    devices = mesh.devices.reshape(16, 2, 4, 4)
    wide = Mesh(devices, DP + SPACE)
    placed = (P(DP, SPACE, None), P(DP, SPACE, None), P())
    return jax.shard_map(
        body,
        mesh=wide,
        in_specs=placed,
        out_specs=(P(DP, SPACE, None), P(DP, SPACE, None), P(None, DP + SPACE)),
        check_vma=False,
    )
```

```python
import math

import jax
import jax.numpy as jnp
from jax import lax
from jax.experimental import pallas as pl
from jax.experimental.pallas import tpu as pltpu
from jax.sharding import Mesh
from jax.sharding import PartitionSpec as P


DP = ("z", "core")
SPACE = ("x", "y")
CH = 192
ROWS = 16
WIDTH = 48
HEIGHT = 256
GROUPS = 3
CELLS = GROUPS * HEIGHT
F32 = jnp.float32
BF16 = jnp.bfloat16
GELU_A = math.sqrt(2.0 / math.pi)
GELU_B = 0.044715
VMEM_LIMIT = 24 * 1024 * 1024
VMEM_MOST = 60 * 1024 * 1024


def gelu(x):
    return x * (0.5 * (1.0 + jnp.tanh(GELU_A * (x + GELU_B * (x * x * x)))))


def gelu_and_slope(x):
    square = x * x
    tanh = jnp.tanh(GELU_A * (x + GELU_B * (x * square)))
    cdf = 0.5 * (1.0 + tanh)
    slope = cdf + (0.5 * x) * ((1.0 - tanh * tanh) * (GELU_A + (3.0 * GELU_A * GELU_B) * square))
    return x * cdf, slope


def dot(a, b):
    return lax.dot_general(a, b, (((1,), (0,)), ((), ())), preferred_element_type=F32)


def dot_t(a, b):
    return lax.dot_general(a, b, (((1,), (1,)), ((), ())), preferred_element_type=F32)


def call(kernel, out_shape, *args, scratch=(), flops=0, moved=0, remain=(), limit=VMEM_LIMIT, apart=0):
    outputs = jax.tree.leaves(out_shape)
    spaces = [pltpu.VMEM] * (len(outputs) - apart) + [pltpu.HBM] * apart
    specs = [pl.BlockSpec(memory_space=space) for space in spaces]
    return pl.pallas_call(
        kernel,
        out_shape=out_shape,
        in_specs=[pl.BlockSpec(memory_space=pltpu.HBM)] * len(remain)
        + [pl.BlockSpec(memory_space=pltpu.VMEM)] * len(args),
        out_specs=jax.tree.unflatten(jax.tree.structure(out_shape), specs),
        scratch_shapes=list(scratch),
        compiler_params=pltpu.CompilerParams(vmem_limit_bytes=limit),
        cost_estimate=pl.CostEstimate(flops=flops, bytes_accessed=moved, transcendentals=0),
    )(*remain, *args)


def shape(*dims, dtype=BF16):
    return jax.ShapeDtypeStruct(dims, dtype)


def pack_kernel(x_hbm, c_hbm, send_hbm, x_ref, c_ref, act_ref, send_ref, sems, send_sems):
    copies = [
        pltpu.make_async_copy(x_hbm, x_ref, sems.at[0]),
        pltpu.make_async_copy(c_hbm, c_ref, sems.at[1]),
    ]
    for copy in copies:
        copy.start()
    copies[0].wait()
    act_ref[...] = gelu(x_ref[0].astype(F32)).astype(BF16)

    def column(load, w):
        pair = load(384 * (w // 2))
        base = 192 * (w % 2)
        return pair[:, base : base + 128], pair[:, base + 128 : base + 192]

    copies[1].wait()
    nothing = jnp.zeros((16, 128), BF16), jnp.zeros((16, 64), BF16)
    act, raw, cot, leaving = [], [], [], []
    for w in range(WIDTH):
        act.append(column(lambda at: act_ref[:, at : at + 384], w))
        raw.append(column(lambda at: x_ref[0, :, at : at + 384], w))
        cot.append(column(lambda at: c_ref[0, :, at : at + 384], w))
    for b in range(16):
        blocks = []
        for g in range(4):
            for a in range(GROUPS):
                w = 16 * a + b
                if g == 0:
                    blocks.append(act[w - 1] if w > 0 else nothing)
                elif g == 1:
                    blocks.append(raw[w])
                elif g == 2:
                    blocks.append(act[w + 1] if w < WIDTH - 1 else nothing)
                else:
                    blocks.append(cot[w])
        for k in range(12):
            send_ref[b, 16 * k : 16 * k + 16, :] = blocks[k][0]
        for k in range(6):
            both = jnp.concatenate([blocks[2 * k][1], blocks[2 * k + 1][1]], axis=1)
            send_ref[b, 192 + 16 * k : 208 + 16 * k, :] = both
        leaving.append(pltpu.make_async_copy(send_ref.at[b], send_hbm.at[b], send_sems.at[b]))
        leaving[b].start()
    for copy in leaving:
        copy.wait()


def shifted_rows(value, by):
    rows = lax.broadcasted_iota(jnp.int32, value.shape, 0)
    rolled = pltpu.roll(value, (-by) % value.shape[0], 0)
    keep = rows != (0 if by < 0 else value.shape[0] - 1)
    return jnp.where(keep, rolled, 0.0)


def spread_conv(padded, w_ref, layer, width, step, transposed):
    totals = []
    for a in range(GROUPS):
        cells, taps = [], []
        for j in range(3):
            src = a + ((1 - j) * step if transposed else (j - 1) * step)
            if not 0 <= src < GROUPS:
                continue
            for i in range(3):
                at = width * (2 - i) if transposed else width * i
                cells.append(padded[src, at : at + HEIGHT, :])
                taps.append(w_ref[9 * layer + 3 * i + j])
        cells = jnp.concatenate(cells, axis=1)
        if transposed:
            totals.append(dot_t(cells, jnp.concatenate(taps, axis=1)))
        else:
            totals.append(dot(cells, jnp.concatenate(taps, axis=0)))
    return totals


def clear_edges(ref, pad):
    for a in range(GROUPS):
        ref[a, 0:pad, :] = jnp.zeros((pad, CH), BF16)
        ref[a, pad + HEIGHT : 2 * pad + HEIGHT, :] = jnp.zeros((pad, CH), BF16)


MAIN_SCRATCH = (
    pltpu.VMEM((16, 288, 128), BF16),
    pltpu.VMEM((CELLS, 3 * CH), BF16),
    pltpu.VMEM((GROUPS, HEIGHT + 32, CH), BF16),
    pltpu.VMEM((GROUPS, HEIGHT + 32, CH), BF16),
    pltpu.VMEM((GROUPS, HEIGHT + 64, CH), BF16),
    pltpu.VMEM((CELLS, CH), F32),
    pltpu.VMEM((CELLS, CH), F32),
    pltpu.SemaphoreType.DMA((4,)),
)


def main_kernel(
    recv_hbm, w_ref, a0_ref, a1_ref, a2_ref, g1_ref, g2_ref, g3_ref, s2_ref, first_hbm,
    recv_ref, a0p, a1p, g2p, g3p, slope1, slope2, sems,
):
    def rows_copy(n, lo, hi):
        part = pltpu.make_async_copy(
            recv_hbm.at[:, lo:hi, :], recv_ref.at[:, lo:hi, :], sems.at[n]
        )
        part.start()
        return part

    first = pltpu.make_async_copy(w_ref.at[0:9], first_hbm, sems.at[3])
    moving = [rows_copy(0, 0, 144), rows_copy(1, 192, 288), rows_copy(2, 144, 192)]

    def block(k):
        lo = recv_ref[:, 16 * k : 16 * k + 16, :].reshape(HEIGHT, 128)
        at = 192 + 16 * (k // 2)
        hi = recv_ref[:, at : at + 16, :].reshape(HEIGHT, 128)[:, 64 * (k % 2) : 64 * (k % 2) + 64]
        return jnp.concatenate([lo, hi], axis=1)

    for ref, pad in ((a1p, 16), (g2p, 16), (g3p, 32)):
        clear_edges(ref, pad)

    first.start()
    moving[0].wait()
    moving[1].wait()
    state = []
    for a in range(GROUPS):
        rows = slice(HEIGHT * a, HEIGHT * (a + 1))
        raw = block(3 + a)
        state.append(raw)
        for j in range(3):
            value = gelu(raw.astype(F32)).astype(BF16) if j == 1 else block(3 * j + a)
            a0_ref[j, rows, :] = value
            a0p[rows, CH * j : CH * (j + 1)] = value

    sums = [[], [], []]
    for a in range(GROUPS):
        rows = slice(HEIGHT * a, HEIGHT * (a + 1))
        for i in range(3):
            taps = jnp.concatenate([w_ref[3 * i + j] for j in range(3)], axis=0)
            sums[i].append(dot(a0p[rows, :], taps))
    moving[2].wait()
    for a in range(GROUPS):
        cot = block(9 + a)
        g3_ref[HEIGHT * a : HEIGHT * (a + 1), :] = cot
        g3p[a, 32 : 32 + HEIGHT, :] = cot
    back = spread_conv(g3p, w_ref, 2, 32, 2, True)
    for a in range(GROUPS):
        rows = slice(HEIGHT * a, HEIGHT * (a + 1))
        branch = shifted_rows(sums[0][a], -1) + sums[1][a] + shifted_rows(sums[2][a], 1)
        state[a] = (state[a].astype(F32) + branch).astype(BF16)
        act, slope = gelu_and_slope(state[a].astype(F32))
        act = act.astype(BF16)
        slope1[rows, :] = slope
        a1_ref[rows, :] = act
        a1p[a, 16 : 16 + HEIGHT, :] = act

    branch = spread_conv(a1p, w_ref, 1, 16, 1, False)
    for a in range(GROUPS):
        rows = slice(HEIGHT * a, HEIGHT * (a + 1))
        state[a] = (state[a].astype(F32) + branch[a]).astype(BF16)
        act, slope = gelu_and_slope(state[a].astype(F32))
        act = act.astype(BF16)
        slope2[rows, :] = slope
        a2_ref[rows, :] = act
        s2_ref[rows, :] = state[a]

    for a in range(GROUPS):
        rows = slice(HEIGHT * a, HEIGHT * (a + 1))
        grad = g3_ref[rows, :].astype(F32) + back[a] * slope2[rows, :]
        grad = grad.astype(BF16)
        g2_ref[rows, :] = grad
        g2p[a, 16 : 16 + HEIGHT, :] = grad

    back = spread_conv(g2p, w_ref, 1, 16, 1, True)
    for a in range(GROUPS):
        rows = slice(HEIGHT * a, HEIGHT * (a + 1))
        grad = g2_ref[rows, :].astype(F32) + back[a] * slope1[rows, :]
        g1_ref[rows, :] = grad.astype(BF16)
    first.wait()


def final_kernel(a2_ref, s2_ref, g1_ref, w_ref, send_ref, a2p):
    clear_edges(a2p, 32)
    for a in range(GROUPS):
        a2p[a, 32 : 32 + HEIGHT, :] = a2_ref[HEIGHT * a : HEIGHT * (a + 1), :]
    branch = spread_conv(a2p, w_ref, 2, 32, 2, False)
    state, grads = [], []
    for a in range(GROUPS):
        rows = slice(HEIGHT * a, HEIGHT * (a + 1))
        state.append(s2_ref[rows, :].astype(F32) + branch[a])
        grads.append(g1_ref[rows, :].astype(F32))

    blocks = grads + state
    for k in range(6):
        send_ref[:, 16 * k : 16 * k + 16, :] = blocks[k][:, 0:128].astype(BF16).reshape(16, 16, 128)
    for k in range(3):
        both = jnp.concatenate([blocks[2 * k][:, 128:192], blocks[2 * k + 1][:, 128:192]], axis=1)
        send_ref[:, 96 + 16 * k : 112 + 16 * k, :] = both.astype(BF16).reshape(16, 16, 128)
    third = jnp.concatenate([grads[2][:, 128:192], jnp.zeros((HEIGHT, 64), F32)], axis=1)
    first = jnp.concatenate([grads[0][:, 128:192], grads[1][:, 128:192]], axis=1)
    parts = [grads[0][:, 0:128], grads[1][:, 0:128], grads[2][:, 0:128], first, third]
    index = lax.broadcasted_iota(jnp.int32, (HEIGHT, 128), 0)
    inner = index % 16
    halo = jnp.zeros((HEIGHT, 128), F32)
    for n, part in enumerate(parts):
        p = 2 * n
        above = pltpu.roll(part, p + 1, 0)
        halo = jnp.where((inner == p) & (index >= 16), above, halo)
        p = 2 * n + 1
        below = pltpu.roll(part, (HEIGHT + p - 16) % HEIGHT, 0)
        halo = jnp.where((inner == p) & (index < HEIGHT - 16), below, halo)
    send_ref[:, 144:160, :] = halo.astype(BF16).reshape(16, 16, 128)


def wgrad_kernel(a0_ref, a1_ref, a2_ref, g1_ref, g2_ref, g3_ref, order_ref, keep_ref, give_ref, gp, acts):
    order = order_ref[...]

    def store(tap, value):
        for ref, at in ((keep_ref, 0), (give_ref, 96)):
            ref[tap, 0:96, :] = value[at : at + 96, 0:128].astype(BF16)
            both = [value[at + 48 * h : at + 48 * h + 48, 128:192] for h in range(2)]
            ref[tap, 96:144, :] = jnp.concatenate(both, axis=1).astype(BF16)

    def spread_grad(layer, act_ref, grad_ref, width, step):
        for a in range(GROUPS):
            gp[a, 0:width, :] = jnp.zeros((width, CH), BF16)
            gp[a, width : width + HEIGHT, :] = grad_ref[HEIGHT * a : HEIGHT * (a + 1), :]
            gp[a, width + HEIGHT : 2 * width + HEIGHT, :] = jnp.zeros((width, CH), BF16)
        acts[...] = dot_t(order, act_ref[...]).astype(BF16)
        for j in range(3):
            off = (1 - j) * step
            sources = [a for a in range(GROUPS) if 0 <= a + off < GROUPS]
            lo, n = sources[0], len(sources)
            left = acts[:, HEIGHT * lo : HEIGHT * (lo + n)]
            for i in range(3):
                at = width * (2 - i)
                right = gp[lo + off : lo + off + n, at : at + HEIGHT, :].reshape(n * HEIGHT, CH)
                store(9 * layer + 3 * i + j, dot(left, right))

    spread_grad(2, a2_ref, g3_ref, 32, 2)
    spread_grad(1, a1_ref, g2_ref, 16, 1)
    shifted = [[], g1_ref[...], []]
    for a in range(GROUPS):
        rows = g1_ref[HEIGHT * a : HEIGHT * (a + 1), :].astype(F32)
        shifted[0].append(shifted_rows(rows, 1).astype(BF16))
        shifted[2].append(shifted_rows(rows, -1).astype(BF16))
    shifted[0] = jnp.concatenate(shifted[0], axis=0)
    shifted[2] = jnp.concatenate(shifted[2], axis=0)
    for j in range(3):
        acts[...] = dot_t(order, a0_ref[j]).astype(BF16)
        for i in range(3):
            store(3 * i + j, dot(acts[...], shifted[i]))


PIECES = (
    ((0, 0, 72),),
    ((0, 72, 144),),
    ((0, 144, 192), (1, 0, 24)),
    ((1, 24, 96),),
    ((1, 96, 168),),
    ((1, 168, 192), (2, 0, 48)),
    ((2, 48, 120),),
    ((2, 120, 192),),
)


def split_kernel(keep_ref, got_ref, part_ref, send_ref):
    send_ref[:, 256:416, :] = part_ref[...]
    total = (keep_ref[...].astype(F32) + got_ref[...].astype(F32)).astype(BF16)
    for h in range(2):
        for t, pieces in enumerate(PIECES):
            for group in range(4):
                parts = []
                for tap in range(7 * group, min(7 * group + 7, 27)):
                    for j, lo, hi in pieces:
                        at = 48 * h + 16 * j
                        if lo < 128:
                            parts.append(total[tap, at : at + 16, lo : min(hi, 128)])
                        if hi > 128:
                            at = 96 + 16 * j
                            first = 64 * h + max(lo, 128) - 128
                            parts.append(total[tap, at : at + 16, first : 64 * h + hi - 128])
                parts.append(jnp.zeros((16, 80 if group == 3 else 8), BF16))
                line = jnp.concatenate(parts, axis=1)
                for n in range(4):
                    at = 64 * group + 16 * n
                    send_ref[8 * h + t, at : at + 16, :] = line[:, 128 * n : 128 * n + 128]


def gather_kernel(got_ref, send_ref, total_ref):
    total = got_ref[0, 0:256, :].astype(F32)
    for s in range(1, 16):
        total = total + got_ref[s, 0:256, :].astype(F32)
    total_ref[...] = total
    for z in range(16):
        send_ref[z] = total_ref[pl.ds(z, 16, stride=16), :].astype(BF16)


def finish_kernel(scale, got_ref, out_ref):
    total = got_ref[0].astype(F32)
    for z in range(1, 16):
        total = total + got_ref[z].astype(F32)
    total = total * scale
    for tap in range(27):
        start = 512 * (tap // 7) + 72 * (tap % 7)
        parts = []
        while sum(part.shape[1] for part in parts) < 72:
            at = start + sum(part.shape[1] for part in parts)
            end = min(start + 72, (at // 128 + 1) * 128)
            row = at // 128
            parts.append(total[row : row + 1, at % 128 : at % 128 + end - at])
        out_ref[tap : tap + 1, :] = parts[0] if len(parts) == 1 else jnp.concatenate(parts, axis=1)


def last_kernel(
    w_hbm, recv_ref, x_ref, out_ref, grad_ref, w_ref, padded, slope_ref, grads_ref, sem
):
    weights = pltpu.make_async_copy(w_hbm, w_ref, sem)
    weights.start()

    def tile(k):
        at = 256 + 16 * k
        return recv_ref[:, at : at + 16, :].reshape(HEIGHT, 128).astype(F32)

    lows = [tile(k) for k in range(6)]
    highs = []
    for k in range(3):
        both = tile(6 + k)
        highs += [both[:, 0:64], both[:, 64:128]]
    halo = tile(9)
    inner = lax.broadcasted_iota(jnp.int32, (HEIGHT, CH), 0) % 16

    def pair(left, right):
        return jnp.concatenate([left, right], axis=1)

    final = [jnp.concatenate([lows[3 + a], highs[3 + a]], axis=1) for a in range(GROUPS)]
    for p in range(WIDTH // 2):
        a, b = (2 * p) // 16, (2 * p) % 16
        left = final[a][16 * b : 16 * b + 16]
        right = final[a][16 * b + 16 : 16 * b + 32]
        out_ref[0, :, 384 * p : 384 * p + 384] = pair(left, right).astype(BF16)

    zeros = jnp.zeros((16, CH), BF16)
    for i in range(3):
        padded[i, 0:16, :] = zeros
        padded[i, 16 + CELLS : 32 + CELLS, :] = zeros
    for a in range(GROUPS):
        at = 16 + HEIGHT * a
        here = jnp.concatenate([lows[a], highs[a]], axis=1)
        grads_ref[HEIGHT * a : HEIGHT * (a + 1), :] = here

        def edge(row, p_lo, p_hi, lane):
            low = pltpu.roll(halo, (row - p_lo) % HEIGHT, 0)
            high = pltpu.roll(halo, (row - p_hi) % HEIGHT, 0)[:, lane : lane + 64]
            return jnp.concatenate([low, high], axis=1)

        hi_slot, lane = ((6, 0), (6, 64), (8, 0))[a]
        above = edge(0, 2 * a, hi_slot, lane)
        below = edge(15, 2 * a + 1, hi_slot + 1, lane)
        after = jnp.where(inner == 15, below, pltpu.roll(here, HEIGHT - 1, 0))
        before = jnp.where(inner == 0, above, pltpu.roll(here, 1, 0))
        padded[0, at : at + HEIGHT, :] = after.astype(BF16)
        padded[1, at : at + HEIGHT, :] = here.astype(BF16)
        padded[2, at : at + HEIGHT, :] = before.astype(BF16)

    for p in range(WIDTH // 2):
        values = x_ref[0, :, 384 * p : 384 * p + 384].astype(F32)
        slope = gelu_and_slope(values)[1]
        slope_ref[32 * p : 32 * p + 16, :] = slope[:, 0:192]
        slope_ref[32 * p + 16 : 32 * p + 32, :] = slope[:, 192:384]

    weights.wait()
    cells, taps = [], []
    for i in range(3):
        for j in range(3):
            at = 16 * (2 - j)
            cells.append(padded[i, at : at + CELLS, :])
            taps.append(w_ref[3 * i + j])
    total = dot_t(jnp.concatenate(cells, axis=1), jnp.concatenate(taps, axis=1))
    result = grads_ref[...] + total * slope_ref[...]
    for p in range(WIDTH // 2):
        left = result[32 * p : 32 * p + 16]
        right = result[32 * p + 16 : 32 * p + 32]
        grad_ref[0, :, 384 * p : 384 * p + 384] = pair(left, right).astype(BF16)


def body(inputs, cotangent, weights):
    count = math.prod(lax.axis_size(axis) for axis in DP + SPACE)
    scale = 1.0 / math.sqrt(count * ROWS * WIDTH)
    core = lax.axis_index("core")

    place = jnp.arange(CH)
    half = (core + place // 96) % 2
    channel = 12 * (place % 16) + 6 * half + 3 * ((place // 48) % 2) + (place // 16) % 3
    order = (channel[:, None] == jnp.arange(CH)[None, :]).astype(BF16)

    send = call(
        pack_kernel,
        shape(16, 288, 128),
        remain=(inputs, cotangent),
        scratch=(
            pltpu.VMEM((1, ROWS, 9216), BF16),
            pltpu.VMEM((1, ROWS, 9216), BF16),
            pltpu.VMEM((ROWS, 9216), BF16),
            pltpu.VMEM((16, 288, 128), BF16),
            pltpu.SemaphoreType.DMA((2,)),
            pltpu.SemaphoreType.DMA((16,)),
        ),
        moved=2500000,
        apart=1,
        limit=VMEM_MOST,
    )
    recv = lax.all_to_all(send, SPACE, 0, 0, tiled=True)
    kernels = weights.reshape(27, CH, CH)
    a0, a1, a2, g1, g2, g3, s2, first = call(
        main_kernel,
        (shape(3, CELLS, CH),) + (shape(CELLS, CH),) * 6 + (shape(9, CH, CH),),
        kernels,
        remain=(recv,),
        scratch=MAIN_SCRATCH,
        apart=1,
        flops=4 * 2 * CELLS * 9 * CH * CH,
        moved=9000000,
    )
    keep, give = call(
        wgrad_kernel,
        (shape(27, 144, 128), shape(27, 144, 128)),
        a0, a1, a2, g1, g2, g3, order,
        scratch=(pltpu.VMEM((GROUPS, HEIGHT + 64, CH), BF16), pltpu.VMEM((CH, CELLS), BF16)),
        flops=3 * 2 * CELLS * 9 * CH * CH,
        moved=7000000,
    )
    got = lax.ppermute(give, "core", [(0, 1), (1, 0)])
    part = call(
        final_kernel,
        shape(16, 160, 128),
        a2, s2, g1, kernels,
        scratch=(pltpu.VMEM((GROUPS, HEIGHT + 64, CH), BF16),),
        flops=2 * CELLS * 9 * CH * CH,
        moved=4500000,
    )
    send = call(split_kernel, shape(16, 416, 128), keep, got, part, moved=5000000)
    back = lax.all_to_all(send, SPACE, 0, 0, tiled=True)
    send = call(
        gather_kernel,
        shape(16, 16, 128),
        back,
        scratch=(pltpu.VMEM((256, 128), F32),),
        moved=2500000,
    )
    got = lax.all_to_all(send, "z", 0, 0, tiled=True)
    weight_grad = call(
        lambda *refs: finish_kernel(scale, *refs), shape(27, 72, dtype=F32), got, moved=150000
    )
    outputs, input_grad = call(
        last_kernel,
        (shape(1, ROWS, 9216), shape(1, ROWS, 9216)),
        back, inputs,
        remain=(first,),
        scratch=(
            pltpu.VMEM((9, CH, CH), BF16),
            pltpu.VMEM((3, CELLS + 32, CH), BF16),
            pltpu.VMEM((CELLS, CH), F32),
            pltpu.VMEM((CELLS, CH), F32),
            pltpu.SemaphoreType.DMA,
        ),
        flops=2 * CELLS * 9 * CH * CH,
        moved=3000000,
    )
    return outputs, input_grad, weight_grad


def solution(mesh):
    devices = mesh.devices.reshape(16, 2, 4, 4)
    wide = Mesh(devices, DP + SPACE)
    placed = (P(DP, SPACE, None), P(DP, SPACE, None), P())
    return jax.shard_map(
        body,
        mesh=wide,
        in_specs=placed,
        out_specs=(P(DP, SPACE, None), P(DP, SPACE, None), P(None, DP + SPACE)),
        check_vma=False,
    )
```

```python
import math

import jax
import jax.numpy as jnp
from jax import lax
from jax.experimental import pallas as pl
from jax.experimental.pallas import tpu as pltpu
from jax.sharding import Mesh
from jax.sharding import PartitionSpec as P


DP = ("z", "core")
SPACE = ("space",)
Z_ORDER = tuple((z + 11) % 16 for z in range(16))
TURNED = tuple(4 * ((s // 4 + 2) % 4) + (s + 2) % 4 for s in range(16))
CH = 192
ROWS = 16
WIDTH = 48
HEIGHT = 256
GROUPS = 3
CELLS = GROUPS * HEIGHT
F32 = jnp.float32
BF16 = jnp.bfloat16
GELU_A = math.sqrt(2.0 / math.pi)
GELU_B = 0.044715
VMEM_LIMIT = 24 * 1024 * 1024
VMEM_MOST = 60 * 1024 * 1024


def gelu(x):
    return x * (0.5 * (1.0 + jnp.tanh(GELU_A * (x + GELU_B * (x * x * x)))))


def gelu_and_slope(x):
    square = x * x
    tanh = jnp.tanh(GELU_A * (x + GELU_B * (x * square)))
    cdf = 0.5 * (1.0 + tanh)
    act = x * cdf
    slope = cdf + (act * (1.0 - cdf)) * (2.0 * GELU_A + (6.0 * GELU_A * GELU_B) * square)
    return act, slope


def dot(a, b):
    return lax.dot_general(a, b, (((1,), (0,)), ((), ())), preferred_element_type=F32)


def dot_t(a, b):
    return lax.dot_general(a, b, (((1,), (1,)), ((), ())), preferred_element_type=F32)


def call(kernel, out_shape, *args, scratch=(), flops=0, moved=0, remain=(), limit=VMEM_LIMIT, apart=0):
    outputs = jax.tree.leaves(out_shape)
    spaces = [pltpu.VMEM] * (len(outputs) - apart) + [pltpu.HBM] * apart
    specs = [pl.BlockSpec(memory_space=space) for space in spaces]
    return pl.pallas_call(
        kernel,
        out_shape=out_shape,
        in_specs=[pl.BlockSpec(memory_space=pltpu.HBM)] * len(remain)
        + [pl.BlockSpec(memory_space=pltpu.VMEM)] * len(args),
        out_specs=jax.tree.unflatten(jax.tree.structure(out_shape), specs),
        scratch_shapes=list(scratch),
        compiler_params=pltpu.CompilerParams(vmem_limit_bytes=limit),
        cost_estimate=pl.CostEstimate(flops=flops, bytes_accessed=moved, transcendentals=0),
    )(*remain, *args)


def plane_exchange(value):
    groups = [list(TURNED)]
    return lax.all_to_all(value, "space", 0, 0, axis_index_groups=groups, tiled=True)


def shape(*dims, dtype=BF16):
    return jax.ShapeDtypeStruct(dims, dtype)


PACK_SCRATCH = (
    pltpu.VMEM((1, ROWS, 9216), BF16),
    pltpu.VMEM((1, ROWS, 9216), BF16),
    pltpu.VMEM((ROWS, 9216), BF16),
    pltpu.VMEM((16, 288, 128), BF16),
    pltpu.SemaphoreType.DMA((6,)),
    pltpu.SemaphoreType.DMA((16,)),
)


def pack_kernel(x_hbm, c_hbm, send_hbm, x_ref, c_ref, act_ref, send_ref, sems, send_sems):
    copies = []
    for n in range(6):
        source, target = ((x_hbm, x_ref), (c_hbm, c_ref))[n // 3]
        part = pl.ds(3072 * (n % 3), 3072)
        copies.append(pltpu.make_async_copy(source.at[:, :, part], target.at[:, :, part], sems.at[n]))
        copies[n].start()
    for n in range(3):
        copies[n].wait()
        part = slice(3072 * n, 3072 * (n + 1))
        act_ref[:, part] = gelu(x_ref[0, :, part].astype(F32)).astype(BF16)

    def column(load, w):
        pair = load(384 * (w // 2))
        base = 192 * (w % 2)
        return pair[:, base : base + 128], pair[:, base + 128 : base + 192]

    for copy in copies[3:]:
        copy.wait()
    nothing = jnp.zeros((16, 128), BF16), jnp.zeros((16, 64), BF16)
    act, raw, cot, leaving = [], [], [], []
    for w in range(WIDTH):
        act.append(column(lambda at: act_ref[:, at : at + 384], w))
        raw.append(column(lambda at: x_ref[0, :, at : at + 384], w))
        cot.append(column(lambda at: c_ref[0, :, at : at + 384], w))
    for b in range(16):
        blocks = []
        for g in range(4):
            for a in range(GROUPS):
                w = 16 * a + b
                if g == 0:
                    blocks.append(act[w - 1] if w > 0 else nothing)
                elif g == 1:
                    blocks.append(raw[w])
                elif g == 2:
                    blocks.append(act[w + 1] if w < WIDTH - 1 else nothing)
                else:
                    blocks.append(cot[w])
        for k in range(12):
            send_ref[b, 16 * k : 16 * k + 16, :] = blocks[k][0]
        for k in range(6):
            both = jnp.concatenate([blocks[2 * k][1], blocks[2 * k + 1][1]], axis=1)
            send_ref[b, 192 + 16 * k : 208 + 16 * k, :] = both
        leaving.append(pltpu.make_async_copy(send_ref.at[b], send_hbm.at[TURNED[b]], send_sems.at[b]))
        leaving[b].start()
    for copy in leaving:
        copy.wait()


def shifted_rows(value, by):
    rows = lax.broadcasted_iota(jnp.int32, value.shape, 0)
    rolled = pltpu.roll(value, (-by) % value.shape[0], 0)
    keep = rows != (0 if by < 0 else value.shape[0] - 1)
    return jnp.where(keep, rolled, 0.0)


def spread_conv_at(a, padded, w_ref, layer, width, step, transposed):
    cells, taps = [], []
    for j in range(3):
        src = a + ((1 - j) * step if transposed else (j - 1) * step)
        if not 0 <= src < GROUPS:
            continue
        for i in range(3):
            at = width * (2 - i) if transposed else width * i
            cells.append(padded[src, at : at + HEIGHT, :])
            taps.append(w_ref[9 * layer + 3 * i + j])
    cells = jnp.concatenate(cells, axis=1)
    if transposed:
        return dot_t(cells, jnp.concatenate(taps, axis=1))
    return dot(cells, jnp.concatenate(taps, axis=0))


def spread_conv(*args):
    return [spread_conv_at(a, *args) for a in range(GROUPS)]


def slabs(ref, at):
    return jnp.concatenate([ref[TURNED[s], at : at + 16, :] for s in range(16)], axis=0)


def clear_edges(ref, pad):
    for a in range(GROUPS):
        ref[a, 0:pad, :] = jnp.zeros((pad, CH), BF16)
        ref[a, pad + HEIGHT : 2 * pad + HEIGHT, :] = jnp.zeros((pad, CH), BF16)


MAIN_SCRATCH = (
    pltpu.VMEM((16, 288, 128), BF16),
    pltpu.VMEM((CELLS, 3 * CH), BF16),
    pltpu.VMEM((GROUPS, HEIGHT + 32, CH), BF16),
    pltpu.VMEM((GROUPS, HEIGHT + 32, CH), BF16),
    pltpu.VMEM((GROUPS, HEIGHT + 64, CH), BF16),
    pltpu.VMEM((CELLS, CH), F32),
    pltpu.VMEM((CELLS, CH), F32),
    pltpu.SemaphoreType.DMA((4,)),
)


def main_kernel(
    recv_hbm, w_ref, a0_ref, a1_ref, a2_ref, g1_ref, g2_ref, g3_ref, s2_ref, first_hbm,
    recv_ref, a0p, a1p, g2p, g3p, slope1, slope2, sems,
):
    def rows_copy(n, lo, hi):
        part = pltpu.make_async_copy(
            recv_hbm.at[:, lo:hi, :], recv_ref.at[:, lo:hi, :], sems.at[n]
        )
        part.start()
        return part

    first = pltpu.make_async_copy(w_ref.at[0:9], first_hbm, sems.at[3])
    moving = [rows_copy(0, 0, 144), rows_copy(1, 192, 288), rows_copy(2, 144, 192)]

    def block(k):
        lo = slabs(recv_ref, 16 * k)
        hi = slabs(recv_ref, 192 + 16 * (k // 2))[:, 64 * (k % 2) : 64 * (k % 2) + 64]
        return jnp.concatenate([lo, hi], axis=1)

    for ref, pad in ((a1p, 16), (g2p, 16), (g3p, 32)):
        clear_edges(ref, pad)

    first.start()
    moving[0].wait()
    moving[1].wait()
    state = []
    for a in range(GROUPS):
        rows = slice(HEIGHT * a, HEIGHT * (a + 1))
        raw = block(3 + a)
        state.append(raw)
        for j in range(3):
            value = gelu(raw.astype(F32)).astype(BF16) if j == 1 else block(3 * j + a)
            a0_ref[j, rows, :] = value
            a0p[rows, CH * j : CH * (j + 1)] = value

    sums = [[], [], []]
    for a in range(GROUPS):
        rows = slice(HEIGHT * a, HEIGHT * (a + 1))
        for i in range(3):
            taps = jnp.concatenate([w_ref[3 * i + j] for j in range(3)], axis=0)
            sums[i].append(dot(a0p[rows, :], taps))
    moving[2].wait()
    for a in range(GROUPS):
        cot = block(9 + a)
        g3_ref[HEIGHT * a : HEIGHT * (a + 1), :] = cot
        g3p[a, 32 : 32 + HEIGHT, :] = cot

    def first_state(a):
        rows = slice(HEIGHT * a, HEIGHT * (a + 1))
        branch = shifted_rows(sums[0][a], -1) + sums[1][a] + shifted_rows(sums[2][a], 1)
        state[a] = (state[a].astype(F32) + branch).astype(BF16)
        act, slope = gelu_and_slope(state[a].astype(F32))
        act = act.astype(BF16)
        slope1[rows, :] = slope
        a1_ref[rows, :] = act
        a1p[a, 16 : 16 + HEIGHT, :] = act

    def second_state(a, branch, back):
        rows = slice(HEIGHT * a, HEIGHT * (a + 1))
        state[a] = (state[a].astype(F32) + branch).astype(BF16)
        act, slope = gelu_and_slope(state[a].astype(F32))
        a2_ref[rows, :] = act.astype(BF16)
        s2_ref[rows, :] = state[a]
        grad = (g3_ref[rows, :].astype(F32) + back * slope).astype(BF16)
        g2_ref[rows, :] = grad
        g2p[a, 16 : 16 + HEIGHT, :] = grad

    def third_grad(a, back):
        rows = slice(HEIGHT * a, HEIGHT * (a + 1))
        grad = g2_ref[rows, :].astype(F32) + back * slope1[rows, :]
        g1_ref[rows, :] = grad.astype(BF16)

    fwd = (a1p, w_ref, 1, 16, 1, False)
    far = (g3p, w_ref, 2, 32, 2, True)
    near = (g2p, w_ref, 1, 16, 1, True)
    back0 = spread_conv_at(0, *far)
    first_state(0)
    first_state(1)
    branch0 = spread_conv_at(0, *fwd)
    first_state(2)
    branch1 = spread_conv_at(1, *fwd)
    second_state(0, branch0, back0)
    back1 = spread_conv_at(1, *far)
    branch2 = spread_conv_at(2, *fwd)
    second_state(1, branch1, back1)
    back2 = spread_conv_at(2, *far)
    near0 = spread_conv_at(0, *near)
    second_state(2, branch2, back2)
    third_grad(0, near0)
    near1 = spread_conv_at(1, *near)
    near2 = spread_conv_at(2, *near)
    third_grad(1, near1)
    third_grad(2, near2)
    first.wait()


def final_kernel(a2_ref, s2_ref, g1_ref, w_ref, send_ref, a2p):
    clear_edges(a2p, 32)
    for a in range(GROUPS):
        a2p[a, 32 : 32 + HEIGHT, :] = a2_ref[HEIGHT * a : HEIGHT * (a + 1), :]
    branch = spread_conv(a2p, w_ref, 2, 32, 2, False)
    state, grads = [], []
    for a in range(GROUPS):
        rows = slice(HEIGHT * a, HEIGHT * (a + 1))
        state.append(s2_ref[rows, :].astype(F32) + branch[a])
        grads.append(g1_ref[rows, :].astype(F32))

    blocks = grads + state
    for k in range(6):
        send_ref[:, 16 * k : 16 * k + 16, :] = blocks[k][:, 0:128].astype(BF16).reshape(16, 16, 128)
    for k in range(3):
        both = jnp.concatenate([blocks[2 * k][:, 128:192], blocks[2 * k + 1][:, 128:192]], axis=1)
        send_ref[:, 96 + 16 * k : 112 + 16 * k, :] = both.astype(BF16).reshape(16, 16, 128)
    third = jnp.concatenate([grads[2][:, 128:192], jnp.zeros((HEIGHT, 64), F32)], axis=1)
    first = jnp.concatenate([grads[0][:, 128:192], grads[1][:, 128:192]], axis=1)
    parts = [grads[0][:, 0:128], grads[1][:, 0:128], grads[2][:, 0:128], first, third]
    index = lax.broadcasted_iota(jnp.int32, (HEIGHT, 128), 0)
    inner = index % 16
    halo = jnp.zeros((HEIGHT, 128), F32)
    for n, part in enumerate(parts):
        p = 2 * n
        above = pltpu.roll(part, p + 1, 0)
        halo = jnp.where((inner == p) & (index >= 16), above, halo)
        p = 2 * n + 1
        below = pltpu.roll(part, (HEIGHT + p - 16) % HEIGHT, 0)
        halo = jnp.where((inner == p) & (index < HEIGHT - 16), below, halo)
    send_ref[:, 144:160, :] = halo.astype(BF16).reshape(16, 16, 128)


def wgrad_kernel(a0_ref, a1_ref, a2_ref, g1_ref, g2_ref, g3_ref, order_ref, keep_ref, give_ref, gp, acts):
    order = order_ref[...]

    def store(tap, value):
        for ref, at in ((keep_ref, 0), (give_ref, 96)):
            ref[tap, 0:96, :] = value[at : at + 96, 0:128].astype(BF16)
            both = [value[at + 48 * h : at + 48 * h + 48, 128:192] for h in range(2)]
            ref[tap, 96:144, :] = jnp.concatenate(both, axis=1).astype(BF16)

    def spread_grad(layer, act_ref, grad_ref, width, step):
        for a in range(GROUPS):
            gp[a, 0:width, :] = jnp.zeros((width, CH), BF16)
            gp[a, width : width + HEIGHT, :] = grad_ref[HEIGHT * a : HEIGHT * (a + 1), :]
            gp[a, width + HEIGHT : 2 * width + HEIGHT, :] = jnp.zeros((width, CH), BF16)
        acts[...] = dot_t(order, act_ref[...]).astype(BF16)
        for j in range(3):
            off = (1 - j) * step
            sources = [a for a in range(GROUPS) if 0 <= a + off < GROUPS]
            lo, n = sources[0], len(sources)
            left = acts[:, HEIGHT * lo : HEIGHT * (lo + n)]
            for i in range(3):
                at = width * (2 - i)
                right = gp[lo + off : lo + off + n, at : at + HEIGHT, :].reshape(n * HEIGHT, CH)
                store(9 * layer + 3 * i + j, dot(left, right))

    spread_grad(2, a2_ref, g3_ref, 32, 2)
    spread_grad(1, a1_ref, g2_ref, 16, 1)
    shifted = [[], g1_ref[...], []]
    for a in range(GROUPS):
        rows = g1_ref[HEIGHT * a : HEIGHT * (a + 1), :].astype(F32)
        shifted[0].append(shifted_rows(rows, 1).astype(BF16))
        shifted[2].append(shifted_rows(rows, -1).astype(BF16))
    shifted[0] = jnp.concatenate(shifted[0], axis=0)
    shifted[2] = jnp.concatenate(shifted[2], axis=0)
    stack = jnp.concatenate([dot_t(order, a0_ref[j]).astype(BF16) for j in range(3)], axis=0)
    for i in range(3):
        value = dot(stack, shifted[i])
        for j in range(3):
            store(3 * i + j, value[CH * j : CH * (j + 1)])


PIECES = (
    ((0, 0, 72),),
    ((0, 72, 144),),
    ((0, 144, 192), (1, 0, 24)),
    ((1, 24, 96),),
    ((1, 96, 168),),
    ((1, 168, 192), (2, 0, 48)),
    ((2, 48, 120),),
    ((2, 120, 192),),
)


def split_kernel(keep_ref, got_ref, part_ref, send_ref):
    for s in range(16):
        send_ref[TURNED[s], 256:416, :] = part_ref[s]

    total = (keep_ref[...].astype(F32) + got_ref[...].astype(F32)).astype(BF16)
    for h in range(2):
        for t, pieces in enumerate(PIECES):
            for group in range(4):
                parts = []
                for tap in range(7 * group, min(7 * group + 7, 27)):
                    for j, lo, hi in pieces:
                        at = 48 * h + 16 * j
                        if lo < 128:
                            parts.append(total[tap, at : at + 16, lo : min(hi, 128)])
                        if hi > 128:
                            at = 96 + 16 * j
                            first = 64 * h + max(lo, 128) - 128
                            parts.append(total[tap, at : at + 16, first : 64 * h + hi - 128])
                parts.append(jnp.zeros((16, 80 if group == 3 else 8), BF16))
                line = jnp.concatenate(parts, axis=1)
                for n in range(4):
                    at = 64 * group + 16 * n
                    send_ref[TURNED[8 * h + t], at : at + 16, :] = line[:, 128 * n : 128 * n + 128]


def gather_kernel(got_ref, send_ref, total_ref):
    total = got_ref[0, 0:256, :].astype(F32)
    for s in range(1, 16):
        total = total + got_ref[s, 0:256, :].astype(F32)
    total_ref[...] = total
    for place, z in enumerate(Z_ORDER):
        send_ref[place] = total_ref[pl.ds(z, 16, stride=16), :].astype(BF16)


def finish_kernel(scale, got_ref, out_ref):
    total = got_ref[0].astype(F32)
    for z in range(1, 16):
        total = total + got_ref[z].astype(F32)
    total = total * scale
    for tap in range(27):
        start = 512 * (tap // 7) + 72 * (tap % 7)
        parts = []
        while sum(part.shape[1] for part in parts) < 72:
            at = start + sum(part.shape[1] for part in parts)
            end = min(start + 72, (at // 128 + 1) * 128)
            row = at // 128
            parts.append(total[row : row + 1, at % 128 : at % 128 + end - at])
        out_ref[tap : tap + 1, :] = parts[0] if len(parts) == 1 else jnp.concatenate(parts, axis=1)


def last_kernel(
    w_hbm, recv_ref, x_ref, out_ref, grad_ref, w_ref, padded, slope_ref, grads_ref, sem
):
    weights = pltpu.make_async_copy(w_hbm, w_ref, sem)
    weights.start()

    def tile(k):
        return slabs(recv_ref, 256 + 16 * k).astype(F32)

    lows = [tile(k) for k in range(6)]
    highs = []
    for k in range(3):
        both = tile(6 + k)
        highs += [both[:, 0:64], both[:, 64:128]]
    halo = tile(9)
    inner = lax.broadcasted_iota(jnp.int32, (HEIGHT, CH), 0) % 16

    def pair(left, right):
        return jnp.concatenate([left, right], axis=1)

    final = [jnp.concatenate([lows[3 + a], highs[3 + a]], axis=1) for a in range(GROUPS)]
    for p in range(WIDTH // 2):
        a, b = (2 * p) // 16, (2 * p) % 16
        left = final[a][16 * b : 16 * b + 16]
        right = final[a][16 * b + 16 : 16 * b + 32]
        out_ref[0, :, 384 * p : 384 * p + 384] = pair(left, right).astype(BF16)

    zeros = jnp.zeros((16, CH), BF16)
    for i in range(3):
        padded[i, 0:16, :] = zeros
        padded[i, 16 + CELLS : 32 + CELLS, :] = zeros
    for a in range(GROUPS):
        at = 16 + HEIGHT * a
        here = jnp.concatenate([lows[a], highs[a]], axis=1)
        grads_ref[HEIGHT * a : HEIGHT * (a + 1), :] = here

        def edge(row, p_lo, p_hi, lane):
            low = pltpu.roll(halo, (row - p_lo) % HEIGHT, 0)
            high = pltpu.roll(halo, (row - p_hi) % HEIGHT, 0)[:, lane : lane + 64]
            return jnp.concatenate([low, high], axis=1)

        hi_slot, lane = ((6, 0), (6, 64), (8, 0))[a]
        above = edge(0, 2 * a, hi_slot, lane)
        below = edge(15, 2 * a + 1, hi_slot + 1, lane)
        after = jnp.where(inner == 15, below, pltpu.roll(here, HEIGHT - 1, 0))
        before = jnp.where(inner == 0, above, pltpu.roll(here, 1, 0))
        padded[0, at : at + HEIGHT, :] = after.astype(BF16)
        padded[1, at : at + HEIGHT, :] = here.astype(BF16)
        padded[2, at : at + HEIGHT, :] = before.astype(BF16)

    for p in range(WIDTH // 2):
        values = x_ref[0, :, 384 * p : 384 * p + 384].astype(F32)
        slope = gelu_and_slope(values)[1]
        slope_ref[32 * p : 32 * p + 16, :] = slope[:, 0:192]
        slope_ref[32 * p + 16 : 32 * p + 32, :] = slope[:, 192:384]

    weights.wait()
    cells, taps = [], []
    for i in range(3):
        for j in range(3):
            at = 16 * (2 - j)
            cells.append(padded[i, at : at + CELLS, :])
            taps.append(w_ref[3 * i + j])
    total = dot_t(jnp.concatenate(cells, axis=1), jnp.concatenate(taps, axis=1))
    result = grads_ref[...] + total * slope_ref[...]
    for p in range(WIDTH // 2):
        left = result[32 * p : 32 * p + 16]
        right = result[32 * p + 16 : 32 * p + 32]
        grad_ref[0, :, 384 * p : 384 * p + 384] = pair(left, right).astype(BF16)


def body(inputs, cotangent, weights):
    count = math.prod(lax.axis_size(axis) for axis in DP + SPACE)
    scale = 1.0 / math.sqrt(count * ROWS * WIDTH)
    core = lax.axis_index("core")

    place = jnp.arange(CH)
    half = (core + place // 96) % 2
    channel = 12 * (place % 16) + 6 * half + 3 * ((place // 48) % 2) + (place // 16) % 3
    order = (channel[:, None] == jnp.arange(CH)[None, :]).astype(BF16)

    send = call(
        pack_kernel,
        shape(16, 288, 128),
        remain=(inputs, cotangent),
        scratch=PACK_SCRATCH,
        moved=2500000,
        apart=1,
        limit=VMEM_MOST,
    )
    recv = plane_exchange(send)
    kernels = weights.reshape(27, CH, CH)
    a0, a1, a2, g1, g2, g3, s2, first = call(
        main_kernel,
        (shape(3, CELLS, CH),) + (shape(CELLS, CH),) * 6 + (shape(9, CH, CH),),
        kernels,
        remain=(recv,),
        scratch=MAIN_SCRATCH,
        apart=1,
        flops=4 * 2 * CELLS * 9 * CH * CH,
        moved=9000000,
    )
    keep, give = call(
        wgrad_kernel,
        (shape(27, 144, 128), shape(27, 144, 128)),
        a0, a1, a2, g1, g2, g3, order,
        scratch=(pltpu.VMEM((GROUPS, HEIGHT + 64, CH), BF16), pltpu.VMEM((CH, CELLS), BF16)),
        flops=3 * 2 * CELLS * 9 * CH * CH,
        moved=7000000,
    )
    got = lax.ppermute(give, "core", [(0, 1), (1, 0)])
    part = call(
        final_kernel,
        shape(16, 160, 128),
        a2, s2, g1, kernels,
        scratch=(pltpu.VMEM((GROUPS, HEIGHT + 64, CH), BF16),),
        flops=2 * CELLS * 9 * CH * CH,
        moved=4500000,
    )
    send = call(split_kernel, shape(16, 416, 128), keep, got, part, moved=5000000)
    back = plane_exchange(send)
    send = call(
        gather_kernel,
        shape(16, 16, 128),
        back,
        scratch=(pltpu.VMEM((256, 128), F32),),
        moved=2500000,
    )
    got = lax.all_to_all(send, "z", 0, 0, axis_index_groups=[list(Z_ORDER)], tiled=True)
    weight_grad = call(
        lambda *refs: finish_kernel(scale, *refs), shape(27, 72, dtype=F32), got, moved=150000
    )
    outputs, input_grad = call(
        last_kernel,
        (shape(1, ROWS, 9216), shape(1, ROWS, 9216)),
        back, inputs,
        remain=(first,),
        scratch=(
            pltpu.VMEM((9, CH, CH), BF16),
            pltpu.VMEM((3, CELLS + 32, CH), BF16),
            pltpu.VMEM((CELLS, CH), F32),
            pltpu.VMEM((CELLS, CH), F32),
            pltpu.SemaphoreType.DMA,
        ),
        flops=2 * CELLS * 9 * CH * CH,
        moved=3000000,
    )
    return outputs, input_grad, weight_grad


def solution(mesh):
    devices = mesh.devices.reshape(16, 2, 16)
    wide = Mesh(devices, DP + SPACE)
    placed = (P(DP, SPACE, None), P(DP, SPACE, None), P())
    return jax.shard_map(
        body,
        mesh=wide,
        in_specs=placed,
        out_specs=(P(DP, SPACE, None), P(DP, SPACE, None), P(None, DP + SPACE)),
        check_vma=False,
    )
```

```python
import math

import jax
import jax.numpy as jnp
from jax import lax
from jax.experimental import pallas as pl
from jax.experimental.pallas import tpu as pltpu
from jax.sharding import Mesh
from jax.sharding import PartitionSpec as P


DP = ("z", "core")
SPACE = ("space",)
Z_ORDER = tuple((z + 11) % 16 for z in range(16))
TURNED = tuple(4 * ((s // 4 + 2) % 4) + (s + 2) % 4 for s in range(16))
CH = 192
ROWS = 16
WIDTH = 48
HEIGHT = 256
GROUPS = 3
CELLS = GROUPS * HEIGHT
F32 = jnp.float32
BF16 = jnp.bfloat16
GELU_A = math.sqrt(2.0 / math.pi)
GELU_B = 0.044715
VMEM_LIMIT = 24 * 1024 * 1024
VMEM_MOST = 60 * 1024 * 1024


def gelu(x):
    return x * (0.5 * (1.0 + jnp.tanh(GELU_A * (x + GELU_B * (x * x * x)))))


def gelu_and_slope(x):
    square = x * x
    tanh = jnp.tanh(GELU_A * (x + GELU_B * (x * square)))
    cdf = 0.5 * (1.0 + tanh)
    act = x * cdf
    slope = cdf + (act * (1.0 - cdf)) * (2.0 * GELU_A + (6.0 * GELU_A * GELU_B) * square)
    return act, slope


def dot(a, b):
    return lax.dot_general(a, b, (((1,), (0,)), ((), ())), preferred_element_type=F32)


def dot_t(a, b):
    return lax.dot_general(a, b, (((1,), (1,)), ((), ())), preferred_element_type=F32)


def call(kernel, out_shape, *args, scratch=(), flops=0, moved=0, remain=(), limit=VMEM_LIMIT, apart=0):
    outputs = jax.tree.leaves(out_shape)
    spaces = [pltpu.VMEM] * (len(outputs) - apart) + [pltpu.HBM] * apart
    specs = [pl.BlockSpec(memory_space=space) for space in spaces]
    return pl.pallas_call(
        kernel,
        out_shape=out_shape,
        in_specs=[pl.BlockSpec(memory_space=pltpu.HBM)] * len(remain)
        + [pl.BlockSpec(memory_space=pltpu.VMEM)] * len(args),
        out_specs=jax.tree.unflatten(jax.tree.structure(out_shape), specs),
        scratch_shapes=list(scratch),
        compiler_params=pltpu.CompilerParams(vmem_limit_bytes=limit),
        cost_estimate=pl.CostEstimate(flops=flops, bytes_accessed=moved, transcendentals=0),
    )(*remain, *args)


def plane_exchange(value):
    groups = [list(TURNED)]
    return lax.all_to_all(value, "space", 0, 0, axis_index_groups=groups, tiled=True)


def shape(*dims, dtype=BF16):
    return jax.ShapeDtypeStruct(dims, dtype)


PACK_SCRATCH = (
    pltpu.VMEM((1, ROWS, 9216), BF16),
    pltpu.VMEM((1, ROWS, 9216), BF16),
    pltpu.VMEM((ROWS, 9216), BF16),
    pltpu.VMEM((16, 288, 128), BF16),
    pltpu.SemaphoreType.DMA((6,)),
    pltpu.SemaphoreType.DMA((16,)),
)


def pack_kernel(x_hbm, c_hbm, send_hbm, x_ref, c_ref, act_ref, send_ref, sems, send_sems):
    copies = []
    for n in range(6):
        source, target = ((x_hbm, x_ref), (c_hbm, c_ref))[n // 3]
        part = pl.ds(3072 * (n % 3), 3072)
        copies.append(pltpu.make_async_copy(source.at[:, :, part], target.at[:, :, part], sems.at[n]))
        copies[n].start()
    for n in range(3):
        copies[n].wait()
        part = slice(3072 * n, 3072 * (n + 1))
        act_ref[:, part] = gelu(x_ref[0, :, part].astype(F32)).astype(BF16)

    def column(load, w):
        pair = load(384 * (w // 2))
        base = 192 * (w % 2)
        return pair[:, base : base + 128], pair[:, base + 128 : base + 192]

    for copy in copies[3:]:
        copy.wait()
    nothing = jnp.zeros((16, 128), BF16), jnp.zeros((16, 64), BF16)
    act, raw, cot, leaving = [], [], [], []
    for w in range(WIDTH):
        act.append(column(lambda at: act_ref[:, at : at + 384], w))
        raw.append(column(lambda at: x_ref[0, :, at : at + 384], w))
        cot.append(column(lambda at: c_ref[0, :, at : at + 384], w))
    for b in range(16):
        blocks = []
        for g in range(4):
            for a in range(GROUPS):
                w = 16 * a + b
                if g == 0:
                    blocks.append(act[w - 1] if w > 0 else nothing)
                elif g == 1:
                    blocks.append(raw[w])
                elif g == 2:
                    blocks.append(act[w + 1] if w < WIDTH - 1 else nothing)
                else:
                    blocks.append(cot[w])
        for k in range(12):
            send_ref[b, 16 * k : 16 * k + 16, :] = blocks[k][0]
        for k in range(6):
            both = jnp.concatenate([blocks[2 * k][1], blocks[2 * k + 1][1]], axis=1)
            send_ref[b, 192 + 16 * k : 208 + 16 * k, :] = both
        leaving.append(pltpu.make_async_copy(send_ref.at[b], send_hbm.at[TURNED[b]], send_sems.at[b]))
        leaving[b].start()
    for copy in leaving:
        copy.wait()


def shifted_rows(value, by):
    rows = lax.broadcasted_iota(jnp.int32, value.shape, 0)
    rolled = pltpu.roll(value, (-by) % value.shape[0], 0)
    keep = rows != (0 if by < 0 else value.shape[0] - 1)
    return jnp.where(keep, rolled, 0.0)


def spread_conv_at(a, padded, w_ref, layer, width, step, transposed):
    cells, taps = [], []
    for j in range(3):
        src = a + ((1 - j) * step if transposed else (j - 1) * step)
        if not 0 <= src < GROUPS:
            continue
        for i in range(3):
            at = width * (2 - i) if transposed else width * i
            cells.append(padded[src, at : at + HEIGHT, :])
            taps.append(w_ref[9 * layer + 3 * i + j])
    cells = jnp.concatenate(cells, axis=1)
    if transposed:
        return dot_t(cells, jnp.concatenate(taps, axis=1))
    return dot(cells, jnp.concatenate(taps, axis=0))


def spread_conv(*args):
    return [spread_conv_at(a, *args) for a in range(GROUPS)]


def slabs(ref, at):
    return jnp.concatenate([ref[TURNED[s], at : at + 16, :] for s in range(16)], axis=0)


def clear_edges(ref, pad):
    for a in range(GROUPS):
        ref[a, 0:pad, :] = jnp.zeros((pad, CH), BF16)
        ref[a, pad + HEIGHT : 2 * pad + HEIGHT, :] = jnp.zeros((pad, CH), BF16)


MAIN_SCRATCH = (
    pltpu.VMEM((16, 288, 128), BF16),
    pltpu.VMEM((CELLS, 3 * CH), BF16),
    pltpu.VMEM((GROUPS, HEIGHT + 32, CH), BF16),
    pltpu.VMEM((GROUPS, HEIGHT + 32, CH), BF16),
    pltpu.VMEM((GROUPS, HEIGHT + 64, CH), BF16),
    pltpu.VMEM((CELLS, CH), F32),
    pltpu.VMEM((CELLS, CH), F32),
    pltpu.SemaphoreType.DMA((4,)),
)


def main_kernel(
    recv_hbm, w_ref, a0_ref, a1_ref, a2_ref, g1_ref, g2_ref, g3_ref, s2_ref, first_hbm,
    recv_ref, a0p, a1p, g2p, g3p, slope1, slope2, sems,
):
    def rows_copy(n, lo, hi):
        part = pltpu.make_async_copy(
            recv_hbm.at[:, lo:hi, :], recv_ref.at[:, lo:hi, :], sems.at[n]
        )
        part.start()
        return part

    first = pltpu.make_async_copy(w_ref.at[0:9], first_hbm, sems.at[3])
    moving = [rows_copy(0, 0, 144), rows_copy(1, 192, 288), rows_copy(2, 144, 192)]

    def block(k):
        lo = slabs(recv_ref, 16 * k)
        hi = slabs(recv_ref, 192 + 16 * (k // 2))[:, 64 * (k % 2) : 64 * (k % 2) + 64]
        return jnp.concatenate([lo, hi], axis=1)

    for ref, pad in ((a1p, 16), (g2p, 16), (g3p, 32)):
        clear_edges(ref, pad)

    first.start()
    moving[0].wait()
    moving[1].wait()
    state = []
    for a in range(GROUPS):
        rows = slice(HEIGHT * a, HEIGHT * (a + 1))
        raw = block(3 + a)
        state.append(raw)
        for j in range(3):
            value = gelu(raw.astype(F32)).astype(BF16) if j == 1 else block(3 * j + a)
            a0_ref[j, rows, :] = value
            a0p[rows, CH * j : CH * (j + 1)] = value

    sums = [[], [], []]
    for a in range(GROUPS):
        rows = slice(HEIGHT * a, HEIGHT * (a + 1))
        for i in range(3):
            taps = jnp.concatenate([w_ref[3 * i + j] for j in range(3)], axis=0)
            sums[i].append(dot(a0p[rows, :], taps))
    moving[2].wait()
    for a in range(GROUPS):
        cot = block(9 + a)
        g3_ref[HEIGHT * a : HEIGHT * (a + 1), :] = cot
        g3p[a, 32 : 32 + HEIGHT, :] = cot

    def first_state(a):
        rows = slice(HEIGHT * a, HEIGHT * (a + 1))
        branch = shifted_rows(sums[0][a], -1) + sums[1][a] + shifted_rows(sums[2][a], 1)
        state[a] = (state[a].astype(F32) + branch).astype(BF16)
        act, slope = gelu_and_slope(state[a].astype(F32))
        act = act.astype(BF16)
        slope1[rows, :] = slope
        a1_ref[rows, :] = act
        a1p[a, 16 : 16 + HEIGHT, :] = act

    def second_state(a, branch, back):
        rows = slice(HEIGHT * a, HEIGHT * (a + 1))
        state[a] = (state[a].astype(F32) + branch).astype(BF16)
        act, slope = gelu_and_slope(state[a].astype(F32))
        a2_ref[rows, :] = act.astype(BF16)
        s2_ref[rows, :] = state[a]
        grad = (g3_ref[rows, :].astype(F32) + back * slope).astype(BF16)
        g2_ref[rows, :] = grad
        g2p[a, 16 : 16 + HEIGHT, :] = grad

    def third_grad(a, back):
        rows = slice(HEIGHT * a, HEIGHT * (a + 1))
        grad = g2_ref[rows, :].astype(F32) + back * slope1[rows, :]
        g1_ref[rows, :] = grad.astype(BF16)

    fwd = (a1p, w_ref, 1, 16, 1, False)
    far = (g3p, w_ref, 2, 32, 2, True)
    near = (g2p, w_ref, 1, 16, 1, True)
    back0 = spread_conv_at(0, *far)
    first_state(0)
    first_state(1)
    branch0 = spread_conv_at(0, *fwd)
    first_state(2)
    branch1 = spread_conv_at(1, *fwd)
    second_state(0, branch0, back0)
    back1 = spread_conv_at(1, *far)
    branch2 = spread_conv_at(2, *fwd)
    second_state(1, branch1, back1)
    back2 = spread_conv_at(2, *far)
    near0 = spread_conv_at(0, *near)
    second_state(2, branch2, back2)
    third_grad(0, near0)
    near1 = spread_conv_at(1, *near)
    near2 = spread_conv_at(2, *near)
    third_grad(1, near1)
    third_grad(2, near2)
    first.wait()


def final_kernel(a2_ref, s2_ref, g1_ref, w_ref, send_ref, halo_ref, a2p):
    clear_edges(a2p, 32)
    for a in range(GROUPS):
        a2p[a, 32 : 32 + HEIGHT, :] = a2_ref[HEIGHT * a : HEIGHT * (a + 1), :]
    branch = spread_conv(a2p, w_ref, 2, 32, 2, False)
    state, grads = [], []
    for a in range(GROUPS):
        rows = slice(HEIGHT * a, HEIGHT * (a + 1))
        state.append(s2_ref[rows, :].astype(F32) + branch[a])
        grads.append(g1_ref[rows, :].astype(F32))

    blocks = grads + state
    for k in range(6):
        send_ref[:, 16 * k : 16 * k + 16, :] = blocks[k][:, 0:128].astype(BF16).reshape(16, 16, 128)
    for k in range(3):
        both = jnp.concatenate([blocks[2 * k][:, 128:192], blocks[2 * k + 1][:, 128:192]], axis=1)
        send_ref[:, 96 + 16 * k : 112 + 16 * k, :] = both.astype(BF16).reshape(16, 16, 128)
    index = lax.broadcasted_iota(jnp.int32, (HEIGHT, 64), 0)
    wide = jnp.zeros((HEIGHT, 64), F32)
    narrow = jnp.zeros((HEIGHT, 16), F32)

    def put(total, part, row, side):
        at = index[:, 0 : part.shape[1]]
        if side == 0:
            moved = pltpu.roll(part, row + 1, 0)
            return jnp.where((at % 16 == row) & (at >= 16), moved, total)
        moved = pltpu.roll(part, HEIGHT + row - 16, 0)
        return jnp.where((at % 16 == row) & (at < HEIGHT - 16), moved, total)

    for n in range(18):
        a, c, side = n // 6, (n // 2) % 3, n % 2
        part = grads[a][:, 64 * c : 64 * c + 64]
        if n < 16:
            wide = put(wide, part, n, side)
            continue
        for q in range(4):
            narrow = put(narrow, part[:, 16 * q : 16 * q + 16], 4 * (n - 16) + q, side)
    halo = jnp.concatenate([wide, narrow, jnp.zeros((HEIGHT, 48), F32)], axis=1)
    halo_ref[...] = halo.astype(BF16).reshape(16, 16, 128)


def wgrad_kernel(a0_ref, a1_ref, a2_ref, g1_ref, g2_ref, g3_ref, order_ref, keep_ref, give_ref, gp, acts):
    order = order_ref[...]

    def store(tap, value):
        for ref, at in ((keep_ref, 0), (give_ref, 96)):
            ref[tap, 0:96, :] = value[at : at + 96, 0:128].astype(BF16)
            both = [value[at + 48 * h : at + 48 * h + 48, 128:192] for h in range(2)]
            ref[tap, 96:144, :] = jnp.concatenate(both, axis=1).astype(BF16)

    def spread_grad(layer, act_ref, grad_ref, width, step):
        for a in range(GROUPS):
            gp[a, 0:width, :] = jnp.zeros((width, CH), BF16)
            gp[a, width : width + HEIGHT, :] = grad_ref[HEIGHT * a : HEIGHT * (a + 1), :]
            gp[a, width + HEIGHT : 2 * width + HEIGHT, :] = jnp.zeros((width, CH), BF16)
        acts[...] = dot_t(order, act_ref[...]).astype(BF16)
        for j in range(3):
            off = (1 - j) * step
            sources = [a for a in range(GROUPS) if 0 <= a + off < GROUPS]
            lo, n = sources[0], len(sources)
            left = acts[:, HEIGHT * lo : HEIGHT * (lo + n)]
            for i in range(3):
                at = width * (2 - i)
                right = gp[lo + off : lo + off + n, at : at + HEIGHT, :].reshape(n * HEIGHT, CH)
                store(9 * layer + 3 * i + j, dot(left, right))

    spread_grad(2, a2_ref, g3_ref, 32, 2)
    spread_grad(1, a1_ref, g2_ref, 16, 1)
    shifted = [[], g1_ref[...], []]
    for a in range(GROUPS):
        rows = g1_ref[HEIGHT * a : HEIGHT * (a + 1), :].astype(F32)
        shifted[0].append(shifted_rows(rows, 1).astype(BF16))
        shifted[2].append(shifted_rows(rows, -1).astype(BF16))
    shifted[0] = jnp.concatenate(shifted[0], axis=0)
    shifted[2] = jnp.concatenate(shifted[2], axis=0)
    stack = jnp.concatenate([dot_t(order, a0_ref[j]).astype(BF16) for j in range(3)], axis=0)
    for i in range(3):
        value = dot(stack, shifted[i])
        for j in range(3):
            store(3 * i + j, value[CH * j : CH * (j + 1)])


PIECES = (
    ((0, 0, 72),),
    ((0, 72, 144),),
    ((0, 144, 192), (1, 0, 24)),
    ((1, 24, 96),),
    ((1, 96, 168),),
    ((1, 168, 192), (2, 0, 48)),
    ((2, 48, 120),),
    ((2, 120, 192),),
)


def split_kernel(keep_ref, got_ref, part_ref, halo_ref, send_ref):
    for s in range(16):
        send_ref[TURNED[s], 256:400, :] = part_ref[s]

    total = (keep_ref[...].astype(F32) + got_ref[...].astype(F32)).astype(BF16)
    for h in range(2):
        for t, pieces in enumerate(PIECES):
            for group in range(4):
                parts = []
                for tap in range(7 * group, min(7 * group + 7, 27)):
                    for j, lo, hi in pieces:
                        at = 48 * h + 16 * j
                        if lo < 128:
                            parts.append(total[tap, at : at + 16, lo : min(hi, 128)])
                        if hi > 128:
                            at = 96 + 16 * j
                            first = 64 * h + max(lo, 128) - 128
                            parts.append(total[tap, at : at + 16, first : 64 * h + hi - 128])
                if group == 3:
                    parts.append(halo_ref[8 * h + t][:, 0:80])
                else:
                    parts.append(jnp.zeros((16, 8), BF16))
                line = jnp.concatenate(parts, axis=1)
                for n in range(4):
                    at = 64 * group + 16 * n
                    send_ref[TURNED[8 * h + t], at : at + 16, :] = line[:, 128 * n : 128 * n + 128]


def gather_kernel(got_ref, send_ref, total_ref):
    total = got_ref[0, 0:256, :].astype(F32)
    for s in range(1, 16):
        total = total + got_ref[s, 0:256, :].astype(F32)
    total_ref[...] = total
    for place, z in enumerate(Z_ORDER):
        send_ref[place] = total_ref[pl.ds(z, 16, stride=16), :].astype(BF16)


def finish_kernel(scale, got_ref, out_ref):
    total = got_ref[0].astype(F32)
    for z in range(1, 16):
        total = total + got_ref[z].astype(F32)
    total = total * scale
    for tap in range(27):
        start = 512 * (tap // 7) + 72 * (tap % 7)
        parts = []
        while sum(part.shape[1] for part in parts) < 72:
            at = start + sum(part.shape[1] for part in parts)
            end = min(start + 72, (at // 128 + 1) * 128)
            row = at // 128
            parts.append(total[row : row + 1, at % 128 : at % 128 + end - at])
        out_ref[tap : tap + 1, :] = parts[0] if len(parts) == 1 else jnp.concatenate(parts, axis=1)


def last_kernel(
    w_hbm, recv_ref, x_ref, out_ref, grad_ref, w_ref, padded, slope_ref, grads_ref, sem
):
    weights = pltpu.make_async_copy(w_hbm, w_ref, sem)
    weights.start()

    def tile(k):
        return slabs(recv_ref, 256 + 16 * k).astype(F32)

    lows = [tile(k) for k in range(6)]
    highs = []
    for k in range(3):
        both = tile(6 + k)
        highs += [both[:, 0:64], both[:, 64:128]]
    halo = slabs(recv_ref, 240).astype(F32)[:, 48:128]
    inner = lax.broadcasted_iota(jnp.int32, (HEIGHT, CH), 0) % 16

    def pair(left, right):
        return jnp.concatenate([left, right], axis=1)

    final = [jnp.concatenate([lows[3 + a], highs[3 + a]], axis=1) for a in range(GROUPS)]
    for p in range(WIDTH // 2):
        a, b = (2 * p) // 16, (2 * p) % 16
        left = final[a][16 * b : 16 * b + 16]
        right = final[a][16 * b + 16 : 16 * b + 32]
        out_ref[0, :, 384 * p : 384 * p + 384] = pair(left, right).astype(BF16)

    zeros = jnp.zeros((16, CH), BF16)
    for i in range(3):
        padded[i, 0:16, :] = zeros
        padded[i, 16 + CELLS : 32 + CELLS, :] = zeros
    for a in range(GROUPS):
        at = 16 + HEIGHT * a
        here = jnp.concatenate([lows[a], highs[a]], axis=1)
        grads_ref[HEIGHT * a : HEIGHT * (a + 1), :] = here

        def edge(row, side):
            parts = []
            for c in range(3):
                n = 6 * a + 2 * c + side
                if n < 16:
                    parts.append(pltpu.roll(halo[:, 0:64], (row - n) % HEIGHT, 0))
                    continue
                for q in range(4):
                    at = 4 * (n - 16) + q
                    parts.append(pltpu.roll(halo[:, 64:80], (row - at) % HEIGHT, 0))
            return jnp.concatenate(parts, axis=1)

        above = edge(0, 0)
        below = edge(15, 1)
        after = jnp.where(inner == 15, below, pltpu.roll(here, HEIGHT - 1, 0))
        before = jnp.where(inner == 0, above, pltpu.roll(here, 1, 0))
        padded[0, at : at + HEIGHT, :] = after.astype(BF16)
        padded[1, at : at + HEIGHT, :] = here.astype(BF16)
        padded[2, at : at + HEIGHT, :] = before.astype(BF16)

    for p in range(WIDTH // 2):
        values = x_ref[0, :, 384 * p : 384 * p + 384].astype(F32)
        slope = gelu_and_slope(values)[1]
        slope_ref[32 * p : 32 * p + 16, :] = slope[:, 0:192]
        slope_ref[32 * p + 16 : 32 * p + 32, :] = slope[:, 192:384]

    weights.wait()
    cells, taps = [], []
    for i in range(3):
        for j in range(3):
            at = 16 * (2 - j)
            cells.append(padded[i, at : at + CELLS, :])
            taps.append(w_ref[3 * i + j])
    total = dot_t(jnp.concatenate(cells, axis=1), jnp.concatenate(taps, axis=1))
    result = grads_ref[...] + total * slope_ref[...]
    for p in range(WIDTH // 2):
        left = result[32 * p : 32 * p + 16]
        right = result[32 * p + 16 : 32 * p + 32]
        grad_ref[0, :, 384 * p : 384 * p + 384] = pair(left, right).astype(BF16)


def body(inputs, cotangent, weights):
    count = math.prod(lax.axis_size(axis) for axis in DP + SPACE)
    scale = 1.0 / math.sqrt(count * ROWS * WIDTH)
    core = lax.axis_index("core")

    place = jnp.arange(CH)
    half = (core + place // 96) % 2
    channel = 12 * (place % 16) + 6 * half + 3 * ((place // 48) % 2) + (place // 16) % 3
    order = (channel[:, None] == jnp.arange(CH)[None, :]).astype(BF16)

    send = call(
        pack_kernel,
        shape(16, 288, 128),
        remain=(inputs, cotangent),
        scratch=PACK_SCRATCH,
        moved=2500000,
        apart=1,
        limit=VMEM_MOST,
    )
    recv = plane_exchange(send)
    kernels = weights.reshape(27, CH, CH)
    a0, a1, a2, g1, g2, g3, s2, first = call(
        main_kernel,
        (shape(3, CELLS, CH),) + (shape(CELLS, CH),) * 6 + (shape(9, CH, CH),),
        kernels,
        remain=(recv,),
        scratch=MAIN_SCRATCH,
        apart=1,
        flops=4 * 2 * CELLS * 9 * CH * CH,
        moved=9000000,
    )
    keep, give = call(
        wgrad_kernel,
        (shape(27, 144, 128), shape(27, 144, 128)),
        a0, a1, a2, g1, g2, g3, order,
        scratch=(pltpu.VMEM((GROUPS, HEIGHT + 64, CH), BF16), pltpu.VMEM((CH, CELLS), BF16)),
        flops=3 * 2 * CELLS * 9 * CH * CH,
        moved=7000000,
    )
    got = lax.ppermute(give, "core", [(0, 1), (1, 0)])
    part, halo = call(
        final_kernel,
        (shape(16, 144, 128), shape(16, 16, 128)),
        a2, s2, g1, kernels,
        scratch=(pltpu.VMEM((GROUPS, HEIGHT + 64, CH), BF16),),
        flops=2 * CELLS * 9 * CH * CH,
        moved=4500000,
    )
    send = call(split_kernel, shape(16, 400, 128), keep, got, part, halo, moved=5000000)
    back = plane_exchange(send)
    send = call(
        gather_kernel,
        shape(16, 16, 128),
        back,
        scratch=(pltpu.VMEM((256, 128), F32),),
        moved=2500000,
    )
    got = lax.all_to_all(send, "z", 0, 0, axis_index_groups=[list(Z_ORDER)], tiled=True)
    weight_grad = call(
        lambda *refs: finish_kernel(scale, *refs), shape(27, 72, dtype=F32), got, moved=150000
    )
    outputs, input_grad = call(
        last_kernel,
        (shape(1, ROWS, 9216), shape(1, ROWS, 9216)),
        back, inputs,
        remain=(first,),
        scratch=(
            pltpu.VMEM((9, CH, CH), BF16),
            pltpu.VMEM((3, CELLS + 32, CH), BF16),
            pltpu.VMEM((CELLS, CH), F32),
            pltpu.VMEM((CELLS, CH), F32),
            pltpu.SemaphoreType.DMA,
        ),
        flops=2 * CELLS * 9 * CH * CH,
        moved=3000000,
    )
    return outputs, input_grad, weight_grad


def solution(mesh):
    devices = mesh.devices.reshape(16, 2, 16)
    wide = Mesh(devices, DP + SPACE)
    placed = (P(DP, SPACE, None), P(DP, SPACE, None), P())
    return jax.shard_map(
        body,
        mesh=wide,
        in_specs=placed,
        out_specs=(P(DP, SPACE, None), P(DP, SPACE, None), P(None, DP + SPACE)),
        check_vma=False,
    )
```

```python
import math

import jax
import jax.numpy as jnp
from jax import lax
from jax.experimental import pallas as pl
from jax.experimental.pallas import tpu as pltpu
from jax.sharding import Mesh
from jax.sharding import PartitionSpec as P


DP = ("z", "core")
SPACE = ("space",)
Z_ORDER = tuple((z + 11) % 16 for z in range(16))
TURNED = tuple(4 * ((s // 4 + 2) % 4) + (s + 2) % 4 for s in range(16))
CH = 192
ROWS = 16
WIDTH = 48
HEIGHT = 256
GROUPS = 3
CELLS = GROUPS * HEIGHT
F32 = jnp.float32
BF16 = jnp.bfloat16
GELU_A = math.sqrt(2.0 / math.pi)
GELU_B = 0.044715
VMEM_LIMIT = 24 * 1024 * 1024
VMEM_MOST = 60 * 1024 * 1024


def gelu(x):
    return x * (0.5 * (1.0 + jnp.tanh(GELU_A * (x + GELU_B * (x * x * x)))))


def gelu_and_slope(x):
    square = x * x
    tanh = jnp.tanh(GELU_A * (x + GELU_B * (x * square)))
    cdf = 0.5 * (1.0 + tanh)
    act = x * cdf
    slope = cdf + (act * (1.0 - cdf)) * (2.0 * GELU_A + (6.0 * GELU_A * GELU_B) * square)
    return act, slope


def dot(a, b):
    return lax.dot_general(a, b, (((1,), (0,)), ((), ())), preferred_element_type=F32)


def dot_t(a, b):
    return lax.dot_general(a, b, (((1,), (1,)), ((), ())), preferred_element_type=F32)


def call(kernel, out_shape, *args, scratch=(), flops=0, moved=0, remain=(), limit=VMEM_LIMIT, apart=0):
    outputs = jax.tree.leaves(out_shape)
    spaces = [pltpu.VMEM] * (len(outputs) - apart) + [pltpu.HBM] * apart
    specs = [pl.BlockSpec(memory_space=space) for space in spaces]
    return pl.pallas_call(
        kernel,
        out_shape=out_shape,
        in_specs=[pl.BlockSpec(memory_space=pltpu.HBM)] * len(remain)
        + [pl.BlockSpec(memory_space=pltpu.VMEM)] * len(args),
        out_specs=jax.tree.unflatten(jax.tree.structure(out_shape), specs),
        scratch_shapes=list(scratch),
        compiler_params=pltpu.CompilerParams(vmem_limit_bytes=limit),
        cost_estimate=pl.CostEstimate(flops=flops, bytes_accessed=moved, transcendentals=0),
    )(*remain, *args)


def plane_exchange(value):
    groups = [list(TURNED)]
    return lax.all_to_all(value, "space", 0, 0, axis_index_groups=groups, tiled=True)


def shape(*dims, dtype=BF16):
    return jax.ShapeDtypeStruct(dims, dtype)


PACK_SCRATCH = (
    pltpu.VMEM((1, ROWS, 9216), BF16),
    pltpu.VMEM((1, ROWS, 9216), BF16),
    pltpu.VMEM((ROWS, 9216), BF16),
    pltpu.VMEM((16, 288, 128), BF16),
    pltpu.SemaphoreType.DMA((6,)),
    pltpu.SemaphoreType.DMA((16,)),
)


def pack_kernel(x_hbm, c_hbm, send_hbm, x_ref, c_ref, act_ref, send_ref, sems, send_sems):
    copies = []
    for n in range(6):
        source, target = ((x_hbm, x_ref), (c_hbm, c_ref))[n // 3]
        part = pl.ds(3072 * (n % 3), 3072)
        copies.append(pltpu.make_async_copy(source.at[:, :, part], target.at[:, :, part], sems.at[n]))
        copies[n].start()
    for n in range(3):
        copies[n].wait()
        part = slice(3072 * n, 3072 * (n + 1))
        act_ref[:, part] = gelu(x_ref[0, :, part].astype(F32)).astype(BF16)

    def column(load, w):
        pair = load(384 * (w // 2))
        base = 192 * (w % 2)
        return pair[:, base : base + 128], pair[:, base + 128 : base + 192]

    for copy in copies[3:]:
        copy.wait()
    nothing = jnp.zeros((16, 128), BF16), jnp.zeros((16, 64), BF16)
    act, raw, cot, leaving = [], [], [], []
    for w in range(WIDTH):
        act.append(column(lambda at: act_ref[:, at : at + 384], w))
        raw.append(column(lambda at: x_ref[0, :, at : at + 384], w))
        cot.append(column(lambda at: c_ref[0, :, at : at + 384], w))
    for b in range(16):
        blocks = []
        for g in range(4):
            for a in range(GROUPS):
                w = 16 * a + b
                if g == 0:
                    blocks.append(act[w - 1] if w > 0 else nothing)
                elif g == 1:
                    blocks.append(raw[w])
                elif g == 2:
                    blocks.append(act[w + 1] if w < WIDTH - 1 else nothing)
                else:
                    blocks.append(cot[w])
        for k in range(12):
            send_ref[b, 16 * k : 16 * k + 16, :] = blocks[k][0]
        for k in range(6):
            both = jnp.concatenate([blocks[2 * k][1], blocks[2 * k + 1][1]], axis=1)
            send_ref[b, 192 + 16 * k : 208 + 16 * k, :] = both
        leaving.append(pltpu.make_async_copy(send_ref.at[b], send_hbm.at[TURNED[b]], send_sems.at[b]))
        leaving[b].start()
    for copy in leaving:
        copy.wait()


def shifted_rows(value, by):
    rows = lax.broadcasted_iota(jnp.int32, value.shape, 0)
    rolled = pltpu.roll(value, (-by) % value.shape[0], 0)
    keep = rows != (0 if by < 0 else value.shape[0] - 1)
    return jnp.where(keep, rolled, 0.0)


def spread_conv_at(a, padded, w_ref, layer, width, step, transposed):
    cells, taps = [], []
    for j in range(3):
        src = a + ((1 - j) * step if transposed else (j - 1) * step)
        if not 0 <= src < GROUPS:
            continue
        for i in range(3):
            at = width * (2 - i) if transposed else width * i
            cells.append(padded[src, at : at + HEIGHT, :])
            taps.append(w_ref[9 * layer + 3 * i + j])
    cells = jnp.concatenate(cells, axis=1)
    if transposed:
        return dot_t(cells, jnp.concatenate(taps, axis=1))
    return dot(cells, jnp.concatenate(taps, axis=0))


def spread_conv(*args):
    return [spread_conv_at(a, *args) for a in range(GROUPS)]


def slabs(ref, at):
    return jnp.concatenate([ref[TURNED[s], at : at + 16, :] for s in range(16)], axis=0)


def clear_edges(ref, pad):
    for a in range(GROUPS):
        ref[a, 0:pad, :] = jnp.zeros((pad, CH), BF16)
        ref[a, pad + HEIGHT : 2 * pad + HEIGHT, :] = jnp.zeros((pad, CH), BF16)


MAIN_SCRATCH = (
    pltpu.VMEM((16, 288, 128), BF16),
    pltpu.VMEM((CELLS, 3 * CH), BF16),
    pltpu.VMEM((GROUPS, HEIGHT + 32, CH), BF16),
    pltpu.VMEM((GROUPS, HEIGHT + 32, CH), BF16),
    pltpu.VMEM((GROUPS, HEIGHT + 64, CH), BF16),
    pltpu.VMEM((CELLS, CH), F32),
    pltpu.VMEM((CELLS, CH), F32),
    pltpu.SemaphoreType.DMA((3,)),
)


def main_kernel(
    recv_hbm, w_ref, a0_ref, a1_ref, a2_ref, g1_ref, g2_ref, g3_ref, s2_ref,
    recv_ref, a0p, a1p, g2p, g3p, slope1, slope2, sems,
):
    def rows_copy(n, lo, hi):
        part = pltpu.make_async_copy(
            recv_hbm.at[:, lo:hi, :], recv_ref.at[:, lo:hi, :], sems.at[n]
        )
        part.start()
        return part

    moving = [rows_copy(0, 0, 144), rows_copy(1, 192, 288), rows_copy(2, 144, 192)]

    def block(k):
        lo = slabs(recv_ref, 16 * k)
        hi = slabs(recv_ref, 192 + 16 * (k // 2))[:, 64 * (k % 2) : 64 * (k % 2) + 64]
        return jnp.concatenate([lo, hi], axis=1)

    for ref, pad in ((a1p, 16), (g2p, 16), (g3p, 32)):
        clear_edges(ref, pad)

    moving[0].wait()
    moving[1].wait()
    state = []
    for a in range(GROUPS):
        rows = slice(HEIGHT * a, HEIGHT * (a + 1))
        raw = block(3 + a)
        state.append(raw)
        for j in range(3):
            value = gelu(raw.astype(F32)).astype(BF16) if j == 1 else block(3 * j + a)
            a0_ref[j, rows, :] = value
            a0p[rows, CH * j : CH * (j + 1)] = value

    sums = [[], [], []]
    for a in range(GROUPS):
        rows = slice(HEIGHT * a, HEIGHT * (a + 1))
        for i in range(3):
            taps = jnp.concatenate([w_ref[3 * i + j] for j in range(3)], axis=0)
            sums[i].append(dot(a0p[rows, :], taps))
    moving[2].wait()
    for a in range(GROUPS):
        cot = block(9 + a)
        g3_ref[HEIGHT * a : HEIGHT * (a + 1), :] = cot
        g3p[a, 32 : 32 + HEIGHT, :] = cot

    def first_state(a):
        rows = slice(HEIGHT * a, HEIGHT * (a + 1))
        branch = shifted_rows(sums[0][a], -1) + sums[1][a] + shifted_rows(sums[2][a], 1)
        state[a] = (state[a].astype(F32) + branch).astype(BF16)
        act, slope = gelu_and_slope(state[a].astype(F32))
        act = act.astype(BF16)
        slope1[rows, :] = slope
        a1_ref[rows, :] = act
        a1p[a, 16 : 16 + HEIGHT, :] = act

    def second_state(a, branch, back):
        rows = slice(HEIGHT * a, HEIGHT * (a + 1))
        state[a] = (state[a].astype(F32) + branch).astype(BF16)
        act, slope = gelu_and_slope(state[a].astype(F32))
        a2_ref[rows, :] = act.astype(BF16)
        s2_ref[rows, :] = state[a]
        grad = (g3_ref[rows, :].astype(F32) + back * slope).astype(BF16)
        g2_ref[rows, :] = grad
        g2p[a, 16 : 16 + HEIGHT, :] = grad

    def third_grad(a, back):
        rows = slice(HEIGHT * a, HEIGHT * (a + 1))
        grad = g2_ref[rows, :].astype(F32) + back * slope1[rows, :]
        g1_ref[rows, :] = grad.astype(BF16)

    fwd = (a1p, w_ref, 1, 16, 1, False)
    far = (g3p, w_ref, 2, 32, 2, True)
    near = (g2p, w_ref, 1, 16, 1, True)
    back0 = spread_conv_at(0, *far)
    first_state(0)
    first_state(1)
    branch0 = spread_conv_at(0, *fwd)
    first_state(2)
    branch1 = spread_conv_at(1, *fwd)
    second_state(0, branch0, back0)
    back1 = spread_conv_at(1, *far)
    branch2 = spread_conv_at(2, *fwd)
    second_state(1, branch1, back1)
    back2 = spread_conv_at(2, *far)
    near0 = spread_conv_at(0, *near)
    second_state(2, branch2, back2)
    third_grad(0, near0)
    near1 = spread_conv_at(1, *near)
    near2 = spread_conv_at(2, *near)
    third_grad(1, near1)
    third_grad(2, near2)


def final_kernel(a2_ref, s2_ref, g1_ref, w_ref, send_ref, halo_ref, first_hbm, a2p, sem):
    first = pltpu.make_async_copy(w_ref.at[0:9], first_hbm, sem)
    first.start()
    clear_edges(a2p, 32)
    for a in range(GROUPS):
        a2p[a, 32 : 32 + HEIGHT, :] = a2_ref[HEIGHT * a : HEIGHT * (a + 1), :]
    branch = spread_conv(a2p, w_ref, 2, 32, 2, False)
    state, grads = [], []
    for a in range(GROUPS):
        rows = slice(HEIGHT * a, HEIGHT * (a + 1))
        state.append(s2_ref[rows, :].astype(F32) + branch[a])
        grads.append(g1_ref[rows, :].astype(F32))

    blocks = grads + state
    for k in range(6):
        send_ref[:, 16 * k : 16 * k + 16, :] = blocks[k][:, 0:128].astype(BF16).reshape(16, 16, 128)
    for k in range(3):
        both = jnp.concatenate([blocks[2 * k][:, 128:192], blocks[2 * k + 1][:, 128:192]], axis=1)
        send_ref[:, 96 + 16 * k : 112 + 16 * k, :] = both.astype(BF16).reshape(16, 16, 128)
    index = lax.broadcasted_iota(jnp.int32, (HEIGHT, 64), 0)
    wide = jnp.zeros((HEIGHT, 64), F32)
    narrow = jnp.zeros((HEIGHT, 16), F32)

    def put(total, part, row, side):
        at = index[:, 0 : part.shape[1]]
        if side == 0:
            moved = pltpu.roll(part, row + 1, 0)
            return jnp.where((at % 16 == row) & (at >= 16), moved, total)
        moved = pltpu.roll(part, HEIGHT + row - 16, 0)
        return jnp.where((at % 16 == row) & (at < HEIGHT - 16), moved, total)

    for n in range(18):
        a, c, side = n // 6, (n // 2) % 3, n % 2
        part = grads[a][:, 64 * c : 64 * c + 64]
        if n < 16:
            wide = put(wide, part, n, side)
            continue
        for q in range(4):
            narrow = put(narrow, part[:, 16 * q : 16 * q + 16], 4 * (n - 16) + q, side)
    halo = jnp.concatenate([wide, narrow, jnp.zeros((HEIGHT, 48), F32)], axis=1)
    halo_ref[...] = halo.astype(BF16).reshape(16, 16, 128)
    first.wait()


def wgrad_kernel(a0_ref, a1_ref, a2_ref, g1_ref, g2_ref, g3_ref, order_ref, keep_ref, give_ref, gp, acts):
    order = order_ref[...]

    def store(tap, value):
        for ref, at in ((keep_ref, 0), (give_ref, 96)):
            ref[tap, 0:96, :] = value[at : at + 96, 0:128].astype(BF16)
            both = [value[at + 48 * h : at + 48 * h + 48, 128:192] for h in range(2)]
            ref[tap, 96:144, :] = jnp.concatenate(both, axis=1).astype(BF16)

    def spread_grad(layer, act_ref, grad_ref, width, step):
        for a in range(GROUPS):
            gp[a, 0:width, :] = jnp.zeros((width, CH), BF16)
            gp[a, width : width + HEIGHT, :] = grad_ref[HEIGHT * a : HEIGHT * (a + 1), :]
            gp[a, width + HEIGHT : 2 * width + HEIGHT, :] = jnp.zeros((width, CH), BF16)
        acts[...] = dot_t(order, act_ref[...]).astype(BF16)
        for j in range(3):
            off = (1 - j) * step
            sources = [a for a in range(GROUPS) if 0 <= a + off < GROUPS]
            lo, n = sources[0], len(sources)
            left = acts[:, HEIGHT * lo : HEIGHT * (lo + n)]
            for i in range(3):
                at = width * (2 - i)
                right = gp[lo + off : lo + off + n, at : at + HEIGHT, :].reshape(n * HEIGHT, CH)
                store(9 * layer + 3 * i + j, dot(left, right))

    spread_grad(2, a2_ref, g3_ref, 32, 2)
    spread_grad(1, a1_ref, g2_ref, 16, 1)
    shifted = [[], g1_ref[...], []]
    for a in range(GROUPS):
        rows = g1_ref[HEIGHT * a : HEIGHT * (a + 1), :].astype(F32)
        shifted[0].append(shifted_rows(rows, 1).astype(BF16))
        shifted[2].append(shifted_rows(rows, -1).astype(BF16))
    shifted[0] = jnp.concatenate(shifted[0], axis=0)
    shifted[2] = jnp.concatenate(shifted[2], axis=0)
    stack = jnp.concatenate([dot_t(order, a0_ref[j]).astype(BF16) for j in range(3)], axis=0)
    for i in range(3):
        value = dot(stack, shifted[i])
        for j in range(3):
            store(3 * i + j, value[CH * j : CH * (j + 1)])


PIECES = (
    ((0, 0, 72),),
    ((0, 72, 144),),
    ((0, 144, 192), (1, 0, 24)),
    ((1, 24, 96),),
    ((1, 96, 168),),
    ((1, 168, 192), (2, 0, 48)),
    ((2, 48, 120),),
    ((2, 120, 192),),
)


def split_kernel(keep_ref, got_ref, part_ref, halo_ref, send_ref):
    for s in range(16):
        send_ref[TURNED[s], 256:400, :] = part_ref[s]

    total = (keep_ref[...].astype(F32) + got_ref[...].astype(F32)).astype(BF16)
    for h in range(2):
        for t, pieces in enumerate(PIECES):
            for group in range(4):
                parts = []
                for tap in range(7 * group, min(7 * group + 7, 27)):
                    for j, lo, hi in pieces:
                        at = 48 * h + 16 * j
                        if lo < 128:
                            parts.append(total[tap, at : at + 16, lo : min(hi, 128)])
                        if hi > 128:
                            at = 96 + 16 * j
                            first = 64 * h + max(lo, 128) - 128
                            parts.append(total[tap, at : at + 16, first : 64 * h + hi - 128])
                if group == 3:
                    parts.append(halo_ref[8 * h + t][:, 0:80])
                else:
                    parts.append(jnp.zeros((16, 8), BF16))
                line = jnp.concatenate(parts, axis=1)
                for n in range(4):
                    at = 64 * group + 16 * n
                    send_ref[TURNED[8 * h + t], at : at + 16, :] = line[:, 128 * n : 128 * n + 128]


def gather_kernel(got_ref, send_ref, total_ref):
    total = got_ref[0, 0:256, :].astype(F32)
    for s in range(1, 16):
        total = total + got_ref[s, 0:256, :].astype(F32)
    total_ref[...] = total
    for place, z in enumerate(Z_ORDER):
        send_ref[place] = total_ref[pl.ds(z, 16, stride=16), :].astype(BF16)


def finish_kernel(scale, got_ref, out_ref):
    total = got_ref[0].astype(F32)
    for z in range(1, 16):
        total = total + got_ref[z].astype(F32)
    total = total * scale
    for tap in range(27):
        start = 512 * (tap // 7) + 72 * (tap % 7)
        parts = []
        while sum(part.shape[1] for part in parts) < 72:
            at = start + sum(part.shape[1] for part in parts)
            end = min(start + 72, (at // 128 + 1) * 128)
            row = at // 128
            parts.append(total[row : row + 1, at % 128 : at % 128 + end - at])
        out_ref[tap : tap + 1, :] = parts[0] if len(parts) == 1 else jnp.concatenate(parts, axis=1)


def last_kernel(
    w_hbm, recv_ref, x_ref, out_ref, grad_ref, w_ref, padded, slope_ref, grads_ref, sem
):
    weights = pltpu.make_async_copy(w_hbm, w_ref, sem)
    weights.start()

    def tile(k):
        return slabs(recv_ref, 256 + 16 * k).astype(F32)

    lows = [tile(k) for k in range(6)]
    highs = []
    for k in range(3):
        both = tile(6 + k)
        highs += [both[:, 0:64], both[:, 64:128]]
    halo = slabs(recv_ref, 240).astype(F32)[:, 48:128]
    inner = lax.broadcasted_iota(jnp.int32, (HEIGHT, CH), 0) % 16

    def pair(left, right):
        return jnp.concatenate([left, right], axis=1)

    final = [jnp.concatenate([lows[3 + a], highs[3 + a]], axis=1) for a in range(GROUPS)]
    for p in range(WIDTH // 2):
        a, b = (2 * p) // 16, (2 * p) % 16
        left = final[a][16 * b : 16 * b + 16]
        right = final[a][16 * b + 16 : 16 * b + 32]
        out_ref[0, :, 384 * p : 384 * p + 384] = pair(left, right).astype(BF16)

    zeros = jnp.zeros((16, CH), BF16)
    for i in range(3):
        padded[i, 0:16, :] = zeros
        padded[i, 16 + CELLS : 32 + CELLS, :] = zeros
    for a in range(GROUPS):
        at = 16 + HEIGHT * a
        here = jnp.concatenate([lows[a], highs[a]], axis=1)
        grads_ref[HEIGHT * a : HEIGHT * (a + 1), :] = here

        def edge(row, side):
            parts = []
            for c in range(3):
                n = 6 * a + 2 * c + side
                if n < 16:
                    parts.append(pltpu.roll(halo[:, 0:64], (row - n) % HEIGHT, 0))
                    continue
                for q in range(4):
                    at = 4 * (n - 16) + q
                    parts.append(pltpu.roll(halo[:, 64:80], (row - at) % HEIGHT, 0))
            return jnp.concatenate(parts, axis=1)

        above = edge(0, 0)
        below = edge(15, 1)
        after = jnp.where(inner == 15, below, pltpu.roll(here, HEIGHT - 1, 0))
        before = jnp.where(inner == 0, above, pltpu.roll(here, 1, 0))
        padded[0, at : at + HEIGHT, :] = after.astype(BF16)
        padded[1, at : at + HEIGHT, :] = here.astype(BF16)
        padded[2, at : at + HEIGHT, :] = before.astype(BF16)

    for p in range(WIDTH // 2):
        values = x_ref[0, :, 384 * p : 384 * p + 384].astype(F32)
        slope = gelu_and_slope(values)[1]
        slope_ref[32 * p : 32 * p + 16, :] = slope[:, 0:192]
        slope_ref[32 * p + 16 : 32 * p + 32, :] = slope[:, 192:384]

    weights.wait()
    cells, taps = [], []
    for i in range(3):
        for j in range(3):
            at = 16 * (2 - j)
            cells.append(padded[i, at : at + CELLS, :])
            taps.append(w_ref[3 * i + j])
    total = dot_t(jnp.concatenate(cells, axis=1), jnp.concatenate(taps, axis=1))
    result = grads_ref[...] + total * slope_ref[...]
    for p in range(WIDTH // 2):
        left = result[32 * p : 32 * p + 16]
        right = result[32 * p + 16 : 32 * p + 32]
        grad_ref[0, :, 384 * p : 384 * p + 384] = pair(left, right).astype(BF16)


def body(inputs, cotangent, weights):
    count = math.prod(lax.axis_size(axis) for axis in DP + SPACE)
    scale = 1.0 / math.sqrt(count * ROWS * WIDTH)
    core = lax.axis_index("core")

    place = jnp.arange(CH)
    half = (core + place // 96) % 2
    channel = 12 * (place % 16) + 6 * half + 3 * ((place // 48) % 2) + (place // 16) % 3
    order = (channel[:, None] == jnp.arange(CH)[None, :]).astype(BF16)

    send = call(
        pack_kernel,
        shape(16, 288, 128),
        remain=(inputs, cotangent),
        scratch=PACK_SCRATCH,
        moved=2500000,
        apart=1,
        limit=VMEM_MOST,
    )
    recv = plane_exchange(send)
    kernels = weights.reshape(27, CH, CH)
    a0, a1, a2, g1, g2, g3, s2 = call(
        main_kernel,
        (shape(3, CELLS, CH),) + (shape(CELLS, CH),) * 6,
        kernels,
        remain=(recv,),
        scratch=MAIN_SCRATCH,
        flops=4 * 2 * CELLS * 9 * CH * CH,
        moved=9000000,
    )
    keep, give = call(
        wgrad_kernel,
        (shape(27, 144, 128), shape(27, 144, 128)),
        a0, a1, a2, g1, g2, g3, order,
        scratch=(pltpu.VMEM((GROUPS, HEIGHT + 64, CH), BF16), pltpu.VMEM((CH, CELLS), BF16)),
        flops=3 * 2 * CELLS * 9 * CH * CH,
        moved=7000000,
    )
    got = lax.ppermute(give, "core", [(0, 1), (1, 0)])
    part, halo, first = call(
        final_kernel,
        (shape(16, 144, 128), shape(16, 16, 128), shape(9, CH, CH)),
        a2, s2, g1, kernels,
        scratch=(pltpu.VMEM((GROUPS, HEIGHT + 64, CH), BF16), pltpu.SemaphoreType.DMA),
        flops=2 * CELLS * 9 * CH * CH,
        moved=4500000,
        apart=1,
    )
    send = call(split_kernel, shape(16, 400, 128), keep, got, part, halo, moved=5000000)
    back = plane_exchange(send)
    send = call(
        gather_kernel,
        shape(16, 16, 128),
        back,
        scratch=(pltpu.VMEM((256, 128), F32),),
        moved=2500000,
    )
    got = lax.all_to_all(send, "z", 0, 0, axis_index_groups=[list(Z_ORDER)], tiled=True)
    weight_grad = call(
        lambda *refs: finish_kernel(scale, *refs), shape(27, 72, dtype=F32), got, moved=150000
    )
    outputs, input_grad = call(
        last_kernel,
        (shape(1, ROWS, 9216), shape(1, ROWS, 9216)),
        back, inputs,
        remain=(first,),
        scratch=(
            pltpu.VMEM((9, CH, CH), BF16),
            pltpu.VMEM((3, CELLS + 32, CH), BF16),
            pltpu.VMEM((CELLS, CH), F32),
            pltpu.VMEM((CELLS, CH), F32),
            pltpu.SemaphoreType.DMA,
        ),
        flops=2 * CELLS * 9 * CH * CH,
        moved=3000000,
    )
    return outputs, input_grad, weight_grad


def solution(mesh):
    devices = mesh.devices.reshape(16, 2, 16)
    wide = Mesh(devices, DP + SPACE)
    placed = (P(DP, SPACE, None), P(DP, SPACE, None), P())
    return jax.shard_map(
        body,
        mesh=wide,
        in_specs=placed,
        out_specs=(P(DP, SPACE, None), P(DP, SPACE, None), P(None, DP + SPACE)),
        check_vma=False,
    )
```

```python
import math

import jax
import jax.numpy as jnp
from jax import lax
from jax.experimental import pallas as pl
from jax.experimental.pallas import tpu as pltpu
from jax.sharding import Mesh
from jax.sharding import PartitionSpec as P


DP = ("z", "core")
SPACE = ("space",)
Z_ORDER = tuple((z + 11) % 16 for z in range(16))
TURNED = tuple(4 * ((s // 4 + 2) % 4) + (s + 2) % 4 for s in range(16))
CH = 192
ROWS = 16
WIDTH = 48
HEIGHT = 256
GROUPS = 3
CELLS = GROUPS * HEIGHT
F32 = jnp.float32
BF16 = jnp.bfloat16
GELU_A = math.sqrt(2.0 / math.pi)
GELU_B = 0.044715
VMEM_LIMIT = 24 * 1024 * 1024
VMEM_MOST = 60 * 1024 * 1024


def gelu(x):
    return x * (0.5 * (1.0 + jnp.tanh(GELU_A * (x + GELU_B * (x * x * x)))))


def gelu_and_slope(x):
    square = x * x
    tanh = jnp.tanh(GELU_A * (x + GELU_B * (x * square)))
    cdf = 0.5 * (1.0 + tanh)
    act = x * cdf
    slope = cdf + (act * (1.0 - cdf)) * (2.0 * GELU_A + (6.0 * GELU_A * GELU_B) * square)
    return act, slope


def dot(a, b):
    return lax.dot_general(a, b, (((1,), (0,)), ((), ())), preferred_element_type=F32)


def dot_t(a, b):
    return lax.dot_general(a, b, (((1,), (1,)), ((), ())), preferred_element_type=F32)


def call(kernel, out_shape, *args, scratch=(), flops=0, moved=0, remain=(), limit=VMEM_LIMIT, apart=0):
    outputs = jax.tree.leaves(out_shape)
    spaces = [pltpu.VMEM] * (len(outputs) - apart) + [pltpu.HBM] * apart
    specs = [pl.BlockSpec(memory_space=space) for space in spaces]
    return pl.pallas_call(
        kernel,
        out_shape=out_shape,
        in_specs=[pl.BlockSpec(memory_space=pltpu.HBM)] * len(remain)
        + [pl.BlockSpec(memory_space=pltpu.VMEM)] * len(args),
        out_specs=jax.tree.unflatten(jax.tree.structure(out_shape), specs),
        scratch_shapes=list(scratch),
        compiler_params=pltpu.CompilerParams(vmem_limit_bytes=limit),
        cost_estimate=pl.CostEstimate(flops=flops, bytes_accessed=moved, transcendentals=0),
    )(*remain, *args)


def plane_exchange(value):
    groups = [list(TURNED)]
    return lax.all_to_all(value, "space", 0, 0, axis_index_groups=groups, tiled=True)


def shape(*dims, dtype=BF16):
    return jax.ShapeDtypeStruct(dims, dtype)


PACK_SCRATCH = (
    pltpu.VMEM((1, ROWS, 9216), BF16),
    pltpu.VMEM((1, ROWS, 9216), BF16),
    pltpu.VMEM((ROWS, 9216), BF16),
    pltpu.VMEM((16, 288, 128), BF16),
    pltpu.SemaphoreType.DMA((6,)),
    pltpu.SemaphoreType.DMA((16,)),
)


def pack_kernel(x_hbm, c_hbm, send_hbm, x_ref, c_ref, act_ref, send_ref, sems, send_sems):
    copies = []
    for n in range(6):
        source, target = ((x_hbm, x_ref), (c_hbm, c_ref))[n // 3]
        part = pl.ds(3072 * (n % 3), 3072)
        copies.append(pltpu.make_async_copy(source.at[:, :, part], target.at[:, :, part], sems.at[n]))
        copies[n].start()
    for n in range(3):
        copies[n].wait()
        part = slice(3072 * n, 3072 * (n + 1))
        act_ref[:, part] = gelu(x_ref[0, :, part].astype(F32)).astype(BF16)

    def column(load, w):
        pair = load(384 * (w // 2))
        base = 192 * (w % 2)
        return pair[:, base : base + 128], pair[:, base + 128 : base + 192]

    for copy in copies[3:]:
        copy.wait()
    nothing = jnp.zeros((16, 128), BF16), jnp.zeros((16, 64), BF16)
    act, raw, cot, leaving = [], [], [], []
    for w in range(WIDTH):
        act.append(column(lambda at: act_ref[:, at : at + 384], w))
        raw.append(column(lambda at: x_ref[0, :, at : at + 384], w))
        cot.append(column(lambda at: c_ref[0, :, at : at + 384], w))
    for b in range(16):
        blocks = []
        for g in range(4):
            for a in range(GROUPS):
                w = 16 * a + b
                if g == 0:
                    blocks.append(act[w - 1] if w > 0 else nothing)
                elif g == 1:
                    blocks.append(raw[w])
                elif g == 2:
                    blocks.append(act[w + 1] if w < WIDTH - 1 else nothing)
                else:
                    blocks.append(cot[w])
        for k in range(12):
            send_ref[b, 16 * k : 16 * k + 16, :] = blocks[k][0]
        for k in range(6):
            both = jnp.concatenate([blocks[2 * k][1], blocks[2 * k + 1][1]], axis=1)
            send_ref[b, 192 + 16 * k : 208 + 16 * k, :] = both
        leaving.append(pltpu.make_async_copy(send_ref.at[b], send_hbm.at[TURNED[b]], send_sems.at[b]))
        leaving[b].start()
    for copy in leaving:
        copy.wait()


def shifted_rows(value, by):
    rows = lax.broadcasted_iota(jnp.int32, value.shape, 0)
    rolled = pltpu.roll(value, (-by) % value.shape[0], 0)
    keep = rows != (0 if by < 0 else value.shape[0] - 1)
    return jnp.where(keep, rolled, 0.0)


def spread_conv_at(a, padded, w_ref, layer, width, step, transposed):
    cells, taps = [], []
    for j in range(3):
        src = a + ((1 - j) * step if transposed else (j - 1) * step)
        if not 0 <= src < GROUPS:
            continue
        for i in range(3):
            at = width * (2 - i) if transposed else width * i
            cells.append(padded[src, at : at + HEIGHT, :])
            taps.append(w_ref[9 * layer + 3 * i + j])
    cells = jnp.concatenate(cells, axis=1)
    if transposed:
        return dot_t(cells, jnp.concatenate(taps, axis=1))
    return dot(cells, jnp.concatenate(taps, axis=0))


def spread_conv(*args):
    return [spread_conv_at(a, *args) for a in range(GROUPS)]


def slabs(ref, at):
    return jnp.concatenate([ref[TURNED[s], at : at + 16, :] for s in range(16)], axis=0)


def clear_edges(ref, pad):
    for a in range(GROUPS):
        ref[a, 0:pad, :] = jnp.zeros((pad, CH), BF16)
        ref[a, pad + HEIGHT : 2 * pad + HEIGHT, :] = jnp.zeros((pad, CH), BF16)


MAIN_SCRATCH = (
    pltpu.VMEM((16, 288, 128), BF16),
    pltpu.VMEM((CELLS, 3 * CH), BF16),
    pltpu.VMEM((GROUPS, HEIGHT + 32, CH), BF16),
    pltpu.VMEM((GROUPS, HEIGHT + 32, CH), BF16),
    pltpu.VMEM((GROUPS, HEIGHT + 64, CH), BF16),
    pltpu.VMEM((CELLS, CH), F32),
    pltpu.VMEM((CELLS, CH), F32),
    pltpu.SemaphoreType.DMA((3,)),
)


def main_kernel(
    recv_hbm, w_ref, a0_ref, a1_ref, a2_ref, g1_ref, g2_ref, g3_ref, s2_ref,
    recv_ref, a0p, a1p, g2p, g3p, slope1, slope2, sems,
):
    def rows_copy(n, lo, hi):
        part = pltpu.make_async_copy(
            recv_hbm.at[:, lo:hi, :], recv_ref.at[:, lo:hi, :], sems.at[n]
        )
        part.start()
        return part

    moving = [rows_copy(0, 0, 144), rows_copy(1, 192, 288)]

    def block(k):
        lo = slabs(recv_ref, 16 * k)
        hi = slabs(recv_ref, 192 + 16 * (k // 2))[:, 64 * (k % 2) : 64 * (k % 2) + 64]
        return jnp.concatenate([lo, hi], axis=1)

    for ref, pad in ((a1p, 16), (g2p, 16), (g3p, 32)):
        clear_edges(ref, pad)

    moving[0].wait()
    moving[1].wait()
    moving.append(rows_copy(2, 144, 192))
    state = []
    for a in range(GROUPS):
        rows = slice(HEIGHT * a, HEIGHT * (a + 1))
        raw = block(3 + a)
        state.append(raw)
        for j in range(3):
            value = gelu(raw.astype(F32)).astype(BF16) if j == 1 else block(3 * j + a)
            a0_ref[j, rows, :] = value
            a0p[rows, CH * j : CH * (j + 1)] = value

    sums = [[], [], []]
    for a in range(GROUPS):
        rows = slice(HEIGHT * a, HEIGHT * (a + 1))
        for i in range(3):
            taps = jnp.concatenate([w_ref[3 * i + j] for j in range(3)], axis=0)
            sums[i].append(dot(a0p[rows, :], taps))
    moving[2].wait()
    for a in range(GROUPS):
        cot = block(9 + a)
        g3_ref[HEIGHT * a : HEIGHT * (a + 1), :] = cot
        g3p[a, 32 : 32 + HEIGHT, :] = cot

    def first_state(a):
        rows = slice(HEIGHT * a, HEIGHT * (a + 1))
        branch = shifted_rows(sums[0][a], -1) + sums[1][a] + shifted_rows(sums[2][a], 1)
        state[a] = (state[a].astype(F32) + branch).astype(BF16)
        act, slope = gelu_and_slope(state[a].astype(F32))
        act = act.astype(BF16)
        slope1[rows, :] = slope
        a1_ref[rows, :] = act
        a1p[a, 16 : 16 + HEIGHT, :] = act

    def second_state(a, branch, back):
        rows = slice(HEIGHT * a, HEIGHT * (a + 1))
        state[a] = (state[a].astype(F32) + branch).astype(BF16)
        act, slope = gelu_and_slope(state[a].astype(F32))
        a2_ref[rows, :] = act.astype(BF16)
        s2_ref[rows, :] = state[a]
        grad = (g3_ref[rows, :].astype(F32) + back * slope).astype(BF16)
        g2_ref[rows, :] = grad
        g2p[a, 16 : 16 + HEIGHT, :] = grad

    def third_grad(a, back):
        rows = slice(HEIGHT * a, HEIGHT * (a + 1))
        grad = g2_ref[rows, :].astype(F32) + back * slope1[rows, :]
        g1_ref[rows, :] = grad.astype(BF16)

    fwd = (a1p, w_ref, 1, 16, 1, False)
    far = (g3p, w_ref, 2, 32, 2, True)
    near = (g2p, w_ref, 1, 16, 1, True)
    back0 = spread_conv_at(0, *far)
    first_state(0)
    first_state(1)
    branch0 = spread_conv_at(0, *fwd)
    first_state(2)
    branch1 = spread_conv_at(1, *fwd)
    second_state(0, branch0, back0)
    back1 = spread_conv_at(1, *far)
    branch2 = spread_conv_at(2, *fwd)
    second_state(1, branch1, back1)
    back2 = spread_conv_at(2, *far)
    near0 = spread_conv_at(0, *near)
    second_state(2, branch2, back2)
    third_grad(0, near0)
    near1 = spread_conv_at(1, *near)
    near2 = spread_conv_at(2, *near)
    third_grad(1, near1)
    third_grad(2, near2)


def final_kernel(a2_ref, s2_ref, g1_ref, w_ref, send_ref, halo_ref, first_hbm, a2p, sem):
    first = pltpu.make_async_copy(w_ref.at[0:9], first_hbm, sem)
    first.start()
    clear_edges(a2p, 32)
    for a in range(GROUPS):
        a2p[a, 32 : 32 + HEIGHT, :] = a2_ref[HEIGHT * a : HEIGHT * (a + 1), :]
    branch = spread_conv(a2p, w_ref, 2, 32, 2, False)
    state, grads = [], []
    for a in range(GROUPS):
        rows = slice(HEIGHT * a, HEIGHT * (a + 1))
        state.append(s2_ref[rows, :].astype(F32) + branch[a])
        grads.append(g1_ref[rows, :].astype(F32))

    blocks = grads + state
    for k in range(6):
        send_ref[:, 16 * k : 16 * k + 16, :] = blocks[k][:, 0:128].astype(BF16).reshape(16, 16, 128)
    for k in range(3):
        both = jnp.concatenate([blocks[2 * k][:, 128:192], blocks[2 * k + 1][:, 128:192]], axis=1)
        send_ref[:, 96 + 16 * k : 112 + 16 * k, :] = both.astype(BF16).reshape(16, 16, 128)
    index = lax.broadcasted_iota(jnp.int32, (HEIGHT, 64), 0)
    wide = jnp.zeros((HEIGHT, 64), F32)
    narrow = jnp.zeros((HEIGHT, 16), F32)

    def put(total, part, row, side):
        at = index[:, 0 : part.shape[1]]
        if side == 0:
            moved = pltpu.roll(part, row + 1, 0)
            return jnp.where((at % 16 == row) & (at >= 16), moved, total)
        moved = pltpu.roll(part, HEIGHT + row - 16, 0)
        return jnp.where((at % 16 == row) & (at < HEIGHT - 16), moved, total)

    for n in range(18):
        a, c, side = n // 6, (n // 2) % 3, n % 2
        part = grads[a][:, 64 * c : 64 * c + 64]
        if n < 16:
            wide = put(wide, part, n, side)
            continue
        for q in range(4):
            narrow = put(narrow, part[:, 16 * q : 16 * q + 16], 4 * (n - 16) + q, side)
    halo = jnp.concatenate([wide, narrow, jnp.zeros((HEIGHT, 48), F32)], axis=1)
    halo_ref[...] = halo.astype(BF16).reshape(16, 16, 128)
    first.wait()


def wgrad_kernel(a0_ref, a1_ref, a2_ref, g1_ref, g2_ref, g3_ref, order_ref, keep_ref, give_ref, gp, acts):
    order = order_ref[...]

    def store(tap, value):
        for ref, at in ((keep_ref, 0), (give_ref, 96)):
            ref[tap, 0:96, :] = value[at : at + 96, 0:128].astype(BF16)
            both = [value[at + 48 * h : at + 48 * h + 48, 128:192] for h in range(2)]
            ref[tap, 96:144, :] = jnp.concatenate(both, axis=1).astype(BF16)

    def spread_grad(layer, act_ref, grad_ref, width, step):
        for a in range(GROUPS):
            gp[a, 0:width, :] = jnp.zeros((width, CH), BF16)
            gp[a, width : width + HEIGHT, :] = grad_ref[HEIGHT * a : HEIGHT * (a + 1), :]
            gp[a, width + HEIGHT : 2 * width + HEIGHT, :] = jnp.zeros((width, CH), BF16)
        acts[...] = dot_t(order, act_ref[...]).astype(BF16)
        for j in range(3):
            off = (1 - j) * step
            sources = [a for a in range(GROUPS) if 0 <= a + off < GROUPS]
            lo, n = sources[0], len(sources)
            left = acts[:, HEIGHT * lo : HEIGHT * (lo + n)]
            for i in range(3):
                at = width * (2 - i)
                right = gp[lo + off : lo + off + n, at : at + HEIGHT, :].reshape(n * HEIGHT, CH)
                store(9 * layer + 3 * i + j, dot(left, right))

    spread_grad(2, a2_ref, g3_ref, 32, 2)
    spread_grad(1, a1_ref, g2_ref, 16, 1)
    shifted = [[], g1_ref[...], []]
    for a in range(GROUPS):
        rows = g1_ref[HEIGHT * a : HEIGHT * (a + 1), :].astype(F32)
        shifted[0].append(shifted_rows(rows, 1).astype(BF16))
        shifted[2].append(shifted_rows(rows, -1).astype(BF16))
    shifted[0] = jnp.concatenate(shifted[0], axis=0)
    shifted[2] = jnp.concatenate(shifted[2], axis=0)
    stack = jnp.concatenate([dot_t(order, a0_ref[j]).astype(BF16) for j in range(3)], axis=0)
    for i in range(3):
        value = dot(stack, shifted[i])
        for j in range(3):
            store(3 * i + j, value[CH * j : CH * (j + 1)])


PIECES = (
    ((0, 0, 72),),
    ((0, 72, 144),),
    ((0, 144, 192), (1, 0, 24)),
    ((1, 24, 96),),
    ((1, 96, 168),),
    ((1, 168, 192), (2, 0, 48)),
    ((2, 48, 120),),
    ((2, 120, 192),),
)


def split_kernel(keep_ref, got_ref, part_ref, halo_ref, send_ref):
    for s in range(16):
        send_ref[TURNED[s], 256:400, :] = part_ref[s]

    total = (keep_ref[...].astype(F32) + got_ref[...].astype(F32)).astype(BF16)
    for h in range(2):
        for t, pieces in enumerate(PIECES):
            for group in range(4):
                parts = []
                for tap in range(7 * group, min(7 * group + 7, 27)):
                    for j, lo, hi in pieces:
                        at = 48 * h + 16 * j
                        if lo < 128:
                            parts.append(total[tap, at : at + 16, lo : min(hi, 128)])
                        if hi > 128:
                            at = 96 + 16 * j
                            first = 64 * h + max(lo, 128) - 128
                            parts.append(total[tap, at : at + 16, first : 64 * h + hi - 128])
                if group == 3:
                    parts.append(halo_ref[8 * h + t][:, 0:80])
                else:
                    parts.append(jnp.zeros((16, 8), BF16))
                line = jnp.concatenate(parts, axis=1)
                for n in range(4):
                    at = 64 * group + 16 * n
                    send_ref[TURNED[8 * h + t], at : at + 16, :] = line[:, 128 * n : 128 * n + 128]


def gather_kernel(got_ref, send_ref, total_ref):
    total = got_ref[0, 0:256, :].astype(F32)
    for s in range(1, 16):
        total = total + got_ref[s, 0:256, :].astype(F32)
    total_ref[...] = total
    for place, z in enumerate(Z_ORDER):
        send_ref[place] = total_ref[pl.ds(z, 16, stride=16), :].astype(BF16)


def finish_kernel(scale, got_ref, out_ref):
    total = got_ref[0].astype(F32)
    for z in range(1, 16):
        total = total + got_ref[z].astype(F32)
    total = total * scale
    for tap in range(27):
        start = 512 * (tap // 7) + 72 * (tap % 7)
        parts = []
        while sum(part.shape[1] for part in parts) < 72:
            at = start + sum(part.shape[1] for part in parts)
            end = min(start + 72, (at // 128 + 1) * 128)
            row = at // 128
            parts.append(total[row : row + 1, at % 128 : at % 128 + end - at])
        out_ref[tap : tap + 1, :] = parts[0] if len(parts) == 1 else jnp.concatenate(parts, axis=1)


def last_kernel(
    w_hbm, recv_ref, x_ref, out_ref, grad_ref, w_ref, padded, slope_ref, grads_ref, sem
):
    weights = pltpu.make_async_copy(w_hbm, w_ref, sem)
    weights.start()

    def tile(k):
        return slabs(recv_ref, 256 + 16 * k).astype(F32)

    lows = [tile(k) for k in range(6)]
    highs = []
    for k in range(3):
        both = tile(6 + k)
        highs += [both[:, 0:64], both[:, 64:128]]
    halo = slabs(recv_ref, 240).astype(F32)[:, 48:128]
    inner = lax.broadcasted_iota(jnp.int32, (HEIGHT, CH), 0) % 16

    def pair(left, right):
        return jnp.concatenate([left, right], axis=1)

    final = [jnp.concatenate([lows[3 + a], highs[3 + a]], axis=1) for a in range(GROUPS)]
    for p in range(WIDTH // 2):
        a, b = (2 * p) // 16, (2 * p) % 16
        left = final[a][16 * b : 16 * b + 16]
        right = final[a][16 * b + 16 : 16 * b + 32]
        out_ref[0, :, 384 * p : 384 * p + 384] = pair(left, right).astype(BF16)

    zeros = jnp.zeros((16, CH), BF16)
    for i in range(3):
        padded[i, 0:16, :] = zeros
        padded[i, 16 + CELLS : 32 + CELLS, :] = zeros
    for a in range(GROUPS):
        at = 16 + HEIGHT * a
        here = jnp.concatenate([lows[a], highs[a]], axis=1)
        grads_ref[HEIGHT * a : HEIGHT * (a + 1), :] = here

        def edge(row, side):
            parts = []
            for c in range(3):
                n = 6 * a + 2 * c + side
                if n < 16:
                    parts.append(pltpu.roll(halo[:, 0:64], (row - n) % HEIGHT, 0))
                    continue
                for q in range(4):
                    at = 4 * (n - 16) + q
                    parts.append(pltpu.roll(halo[:, 64:80], (row - at) % HEIGHT, 0))
            return jnp.concatenate(parts, axis=1)

        above = edge(0, 0)
        below = edge(15, 1)
        after = jnp.where(inner == 15, below, pltpu.roll(here, HEIGHT - 1, 0))
        before = jnp.where(inner == 0, above, pltpu.roll(here, 1, 0))
        padded[0, at : at + HEIGHT, :] = after.astype(BF16)
        padded[1, at : at + HEIGHT, :] = here.astype(BF16)
        padded[2, at : at + HEIGHT, :] = before.astype(BF16)

    for p in range(WIDTH // 2):
        values = x_ref[0, :, 384 * p : 384 * p + 384].astype(F32)
        slope = gelu_and_slope(values)[1]
        slope_ref[32 * p : 32 * p + 16, :] = slope[:, 0:192]
        slope_ref[32 * p + 16 : 32 * p + 32, :] = slope[:, 192:384]

    weights.wait()
    cells, taps = [], []
    for i in range(3):
        for j in range(3):
            at = 16 * (2 - j)
            cells.append(padded[i, at : at + CELLS, :])
            taps.append(w_ref[3 * i + j])
    total = dot_t(jnp.concatenate(cells, axis=1), jnp.concatenate(taps, axis=1))
    result = grads_ref[...] + total * slope_ref[...]
    for p in range(WIDTH // 2):
        left = result[32 * p : 32 * p + 16]
        right = result[32 * p + 16 : 32 * p + 32]
        grad_ref[0, :, 384 * p : 384 * p + 384] = pair(left, right).astype(BF16)


def body(inputs, cotangent, weights):
    count = math.prod(lax.axis_size(axis) for axis in DP + SPACE)
    scale = 1.0 / math.sqrt(count * ROWS * WIDTH)
    core = lax.axis_index("core")

    place = jnp.arange(CH)
    half = (core + place // 96) % 2
    channel = 12 * (place % 16) + 6 * half + 3 * ((place // 48) % 2) + (place // 16) % 3
    order = (channel[:, None] == jnp.arange(CH)[None, :]).astype(BF16)

    send = call(
        pack_kernel,
        shape(16, 288, 128),
        remain=(inputs, cotangent),
        scratch=PACK_SCRATCH,
        moved=2500000,
        apart=1,
        limit=VMEM_MOST,
    )
    recv = plane_exchange(send)
    kernels = weights.reshape(27, CH, CH)
    a0, a1, a2, g1, g2, g3, s2 = call(
        main_kernel,
        (shape(3, CELLS, CH),) + (shape(CELLS, CH),) * 6,
        kernels,
        remain=(recv,),
        scratch=MAIN_SCRATCH,
        flops=4 * 2 * CELLS * 9 * CH * CH,
        moved=9000000,
    )
    keep, give = call(
        wgrad_kernel,
        (shape(27, 144, 128), shape(27, 144, 128)),
        a0, a1, a2, g1, g2, g3, order,
        scratch=(pltpu.VMEM((GROUPS, HEIGHT + 64, CH), BF16), pltpu.VMEM((CH, CELLS), BF16)),
        flops=3 * 2 * CELLS * 9 * CH * CH,
        moved=7000000,
    )
    got = lax.ppermute(give, "core", [(0, 1), (1, 0)])
    part, halo, first = call(
        final_kernel,
        (shape(16, 144, 128), shape(16, 16, 128), shape(9, CH, CH)),
        a2, s2, g1, kernels,
        scratch=(pltpu.VMEM((GROUPS, HEIGHT + 64, CH), BF16), pltpu.SemaphoreType.DMA),
        flops=2 * CELLS * 9 * CH * CH,
        moved=4500000,
        apart=1,
    )
    send = call(split_kernel, shape(16, 400, 128), keep, got, part, halo, moved=5000000)
    back = plane_exchange(send)
    send = call(
        gather_kernel,
        shape(16, 16, 128),
        back,
        scratch=(pltpu.VMEM((256, 128), F32),),
        moved=2500000,
    )
    got = lax.all_to_all(send, "z", 0, 0, axis_index_groups=[list(Z_ORDER)], tiled=True)
    weight_grad = call(
        lambda *refs: finish_kernel(scale, *refs), shape(27, 72, dtype=F32), got, moved=150000
    )
    outputs, input_grad = call(
        last_kernel,
        (shape(1, ROWS, 9216), shape(1, ROWS, 9216)),
        back, inputs,
        remain=(first,),
        scratch=(
            pltpu.VMEM((9, CH, CH), BF16),
            pltpu.VMEM((3, CELLS + 32, CH), BF16),
            pltpu.VMEM((CELLS, CH), F32),
            pltpu.VMEM((CELLS, CH), F32),
            pltpu.SemaphoreType.DMA,
        ),
        flops=2 * CELLS * 9 * CH * CH,
        moved=3000000,
    )
    return outputs, input_grad, weight_grad


def solution(mesh):
    devices = mesh.devices.reshape(16, 2, 16)
    wide = Mesh(devices, DP + SPACE)
    placed = (P(DP, SPACE, None), P(DP, SPACE, None), P())
    return jax.shard_map(
        body,
        mesh=wide,
        in_specs=placed,
        out_specs=(P(DP, SPACE, None), P(DP, SPACE, None), P(None, DP + SPACE)),
        check_vma=False,
    )
```
